128 devices in a mesh: dom: 16 (over z, x), work: 8 (over y, core).
Axes of the slice: x: 4, y: 4, z: 4, core: 2. Of those that a mesh axis runs over, the one named last changes fastest.
Arguments:
- entity_rows: float32 [16384, 512], P(('dom', 'work')), may hold values from -1.2 to 1.2
- adagrad_state: float32 [16384], P(('dom', 'work')), may hold values from 0.005 to 0.05
- relations: float32 [4096, 512], replicated, may hold values from -6 to 6
- hub_part: int32 [1], replicated, may hold values from 0 to 15
- requests: int32 [128, 512], P(('dom', 'work')), may hold values from 0 to 127, as said below
- source_slot: int32 [256, 1024], P(('dom', 'work')), may hold values from 0 to 1535
- relation_ids: int32 [256, 1024], P(('dom', 'work')), may hold values from 0 to 4095
- target_slot: int32 [256, 1024], P(('dom', 'work')), may hold values from 0 to 1535
- negative_slot: int32 [256, 2, 1024], P(('dom', 'work')), may hold values from 0 to 1535
Outputs:
- new_rows: float32 [16384, 512], P(('dom', 'work'))
- new_state: float32 [16384], P(('dom', 'work'))
The draws below stay inside these ranges and needn't reach their ends.
Inputs may be any that keep to these rules, and one draw needn't show every extreme that they name: The 4 rows that one device requests from one owner are distinct.
All inputs are finite; a program needn't handle non-finite values.
Results may differ from the reference program's by a relative error of at most 0.0003.
Values sent between devices are 32-bit elements; how exact they have to be, the bound alone decides.
A program may use at most 128 MiB of HBM per device.

```python
import math
import jax
import jax.numpy as jnp
import numpy as np
from jax import lax

D = 512
RELS = 4096
NEG = 1024
BUCKETS = 2
BEDGE = 1024
ROWS_DEV = 128
CAP = 4
OWNERS = 128
ENTITIES = 16384
HUBROWS = 1024
N_DOM = 16


def pick_slots(key, dims_out):
    key_coin, key_hub, key_far = jax.random.split(key, 3)
    coin_flip = jax.random.randint(key_coin, dims_out, 0, 2)
    hub_pick = jax.random.randint(key_hub, dims_out, 0, HUBROWS)
    far_pick = HUBROWS + jax.random.randint(key_far, dims_out, 0, OWNERS * CAP)
    return jnp.where(coin_flip == 1, hub_pick, far_pick).astype(jnp.int32)


def draw_requests(key, part):
    key = jax.random.fold_in(key, 11)
    base_rows = jnp.tile(jnp.arange(ROWS_DEV, dtype=jnp.int32)[None, :], (OWNERS * OWNERS, 1))
    shuffled = jax.random.permutation(key, base_rows, axis=1, independent=True)
    return shuffled[:, :CAP].reshape(OWNERS, OWNERS * CAP).astype(jnp.int32)


def draw_source_slot(key, part):
    key = jax.random.fold_in(key, 21)
    return pick_slots(key, (OWNERS * BUCKETS, BEDGE))


def draw_target_slot(key, part):
    key = jax.random.fold_in(key, 22)
    return pick_slots(key, (OWNERS * BUCKETS, BEDGE))


def draw_negative_slot(key, part):
    key = jax.random.fold_in(key, 23)
    return pick_slots(key, (OWNERS * BUCKETS, 2, NEG))


def set_ends(result, key, least, high):
    shape = result.shape
    spot = [jax.random.randint(jax.random.fold_in(key, axis), (), 0, shape[axis]) for axis in range(len(shape))]
    result = result.at[tuple(spot)].set(least)
    longest = shape.index(max(shape))
    spot[longest] = (spot[longest] + 1) % shape[longest]
    return result.at[tuple(spot)].set(high)


def steps_of(own_key, dims, pieces, smallest, top_value):
    def one(axis_at, blocks):
        steps = jax.random.uniform(jax.random.fold_in(jax.random.fold_in(own_key, 6), axis_at), (blocks,), jnp.float32, smallest / len(pieces), top_value / len(pieces))
        return jnp.repeat(jnp.exp(steps), dims[axis_at] // blocks).reshape((-1,) + (1,) * (len(dims) - axis_at - 1))

    level = one(*pieces[0])
    for cut in pieces[1:]:
        level = level * one(*cut)
    return level


def rank_bounds(amount, lean):
    portions = [(1 << 20) // math.isqrt(standing ** lean) + 1 for standing in range(1, amount + 1)]
    deviation = 1 + sum(portions) // (1 << 30)
    return np.cumsum(np.array([max(1, weight // deviation) for weight in portions]))


def ranked(rng, dims, amount, skew):
    grid = rank_bounds(amount, skew)
    pick = jax.random.randint(jax.random.fold_in(rng, 1), dims, 0, int(grid[amount - 1]))
    grade = jnp.searchsorted(jnp.asarray(grid, jnp.int32), pick, side="right")
    return jax.random.permutation(jax.random.fold_in(rng, 2), amount)[grade].astype(jnp.int32)


def bell_draw(key, extent, width, bound, shards=(), held_as=jnp.bfloat16):
    result = width * jax.random.normal(key, extent, jnp.float32)
    if shards:
        result = result * steps_of(key, extent, shards, -0.22, 0.18)
    return jnp.clip(result, -bound, bound).astype(held_as)


def setup_inputs(seed: int = 0) -> dict:
    seeds = jax.random.split(jax.random.key(seed), 10)
    return {
        "entity_rows": bell_draw(seeds[0], (ENTITIES, D), 0.2, 1.2, ((0, 128),), jnp.float32),
        "adagrad_state": jnp.clip(jnp.exp(math.log(0.05) - 2.3025851 * jax.random.uniform(seeds[1], (ENTITIES,), jnp.float32) ** steps_of(seeds[1], (ENTITIES,), ((0, 128),), -0.2, 0.2)), 0.005, 0.05),
        "relations": bell_draw(seeds[2], (RELS, D), 1.0, 6.0, (), jnp.float32),
        "hub_part": jax.random.randint(seeds[3], (1,), 0, N_DOM).astype(jnp.int32),
        "requests": draw_requests(jax.random.fold_in(seeds[9], 71), 0),
        "source_slot": draw_source_slot(jax.random.fold_in(seeds[9], 71), 0),
        "relation_ids": set_ends(ranked(seeds[6], (OWNERS * BUCKETS, BEDGE), RELS, 2), jax.random.fold_in(seeds[6], 3), 0, RELS - 1).astype(jnp.int32),
        "target_slot": draw_target_slot(jax.random.fold_in(seeds[9], 71), 0),
        "negative_slot": draw_negative_slot(jax.random.fold_in(seeds[9], 71), 0),
    }


def bucket_loss(working, relations, source, relation, target, negatives):
    half_width = working.shape[1] // 2
    head_rows = working[source]
    tail_rows = working[target]
    rel_rows = relations[relation]
    head_re, head_im = (head_rows[:, :half_width], head_rows[:, half_width:])
    tail_re, tail_im = (tail_rows[:, :half_width], tail_rows[:, half_width:])
    rel_re, rel_im = (rel_rows[:, :half_width], rel_rows[:, half_width:])
    query = jnp.concatenate([head_re * rel_re - head_im * rel_im, head_re * rel_im + head_im * rel_re], axis=1)
    mirror = jnp.concatenate([rel_re * tail_re + rel_im * tail_im, rel_re * tail_im - rel_im * tail_re], axis=1)
    positive = lax.optimization_barrier(jnp.sum(query * tail_rows, axis=1))
    tail_scores = jnp.einsum('ed,nd->en', query, working[negatives[1]], precision=lax.Precision.HIGHEST)
    head_scores = jnp.einsum('ed,nd->en', mirror, working[negatives[0]], precision=lax.Precision.HIGHEST)
    neg_count = negatives.shape[1]
    return jnp.sum(jax.nn.softplus(-positive)) + (jnp.sum(jax.nn.softplus(tail_scores)) + jnp.sum(jax.nn.softplus(head_scores))) / neg_count

def total_loss(working, relations, source, relation, target, negatives):
    totals = jnp.float32(0.0)
    for bucket in range(source.shape[0]):
        totals = totals + bucket_loss(working, relations, source[bucket], relation[bucket], target[bucket], negatives[bucket])
    return totals

def reference(entity_rows, adagrad_state, relations, hub_part, requests, source_slot, relation_ids, target_slot, negative_slot):
    hub_root = hub_part[0].astype(jnp.int32)
    hub_start = (hub_root * HUBROWS).astype(jnp.int32)
    hub_block = lax.dynamic_slice_in_dim(entity_rows, hub_start, HUBROWS, 0)
    hub_ids = hub_start + jnp.arange(HUBROWS, dtype=jnp.int32)
    peer_base = (jnp.arange(OWNERS, dtype=jnp.int32) * ROWS_DEV)[:, None]
    sources = source_slot.reshape(OWNERS, BUCKETS, BEDGE)
    kinds = relation_ids.reshape(OWNERS, BUCKETS, BEDGE)
    targets = target_slot.reshape(OWNERS, BUCKETS, BEDGE)
    negatives = negative_slot.reshape(OWNERS, BUCKETS, 2, NEG)

    def one_device(totals, inputs):
        request_rows, source, relation, target, negative = inputs
        global_ids = (request_rows.reshape(OWNERS, CAP) + peer_base).reshape(-1).astype(jnp.int32)
        working = jnp.concatenate([hub_block, entity_rows[global_ids]], axis=0)
        gradient = jax.grad(total_loss)(working, relations, source, relation, target, negative)
        row_ids = jnp.concatenate([hub_ids, global_ids], axis=0)
        return (totals.at[row_ids].add(gradient), None)
    gradient, _ = lax.scan(one_device, jnp.zeros_like(entity_rows), (requests, sources, kinds, targets, negatives))
    new_state = adagrad_state + lax.optimization_barrier(jnp.mean(gradient * gradient, axis=1))
    new_rows = entity_rows - 0.1 * gradient / (jnp.sqrt(new_state)[:, None] + 1e-10)
    return (new_rows, new_state)
```

```python
import functools
import jax
import jax.numpy as jnp
from jax import lax
from jax.experimental import pallas as pl
from jax.experimental.pallas import tpu as pltpu
from jax.sharding import PartitionSpec as P

F32 = jnp.float32
BF16 = jnp.bfloat16
NT = (((1,), (1,)), ((), ()))


def train_kernel(tiles, src_s, tgt_s, w_ref, rel_ref, src_v, tgt_v, neg_ref,
                 hub_out, far_out,
                 wb, wbt, cnt, acc, hlin, tlin, qf, rhs, lhs, rlo, dneg):
    step = pl.program_id(0)
    edges = rel_ref.shape[0]
    slots = wb.shape[0]
    hub = hub_out.shape[0]
    negs = neg_ref.shape[2]

    @pl.when(step == 0)
    def _():
        for c in range(4):
            part = w_ref[pl.ds(c, slots, stride=4), :]
            wb[:, c * 128:(c + 1) * 128] = part.astype(BF16)
            wbt[c * 128:(c + 1) * 128, :] = part.T.astype(BF16)
        acc[...] = jnp.zeros_like(acc)

    @pl.when(lax.rem(step, tiles) == 0)
    def _():
        groups = slots // 128
        high = lax.broadcasted_iota(jnp.int32, (16, negs), 0)
        low = lax.broadcasted_iota(jnp.int32, (128, negs), 0)
        for side in range(2):
            slot = neg_ref[0, side:side + 1, :]
            top = (high == lax.shift_right_logical(slot, 7)).astype(F32).astype(BF16)
            end = (low == jnp.bitwise_and(slot, 127)).astype(F32).astype(BF16)
            table = lax.dot_general(end, top, NT, preferred_element_type=F32) * (0.5 / negs)
            for g in range(groups):
                cnt[side, g * 128:(g + 1) * 128, :] = jnp.broadcast_to(table[:, g:g + 1], (128, 128))

    base = step * edges

    def gather(e, carry):
        s = src_s[base + e]
        t = tgt_s[base + e]
        hlin[pl.ds(pl.multiple_of(e * 4, 4), 4), :] = w_ref[pl.ds(pl.multiple_of(s * 4, 4), 4), :]
        tlin[pl.ds(pl.multiple_of(e * 4, 4), 4), :] = w_ref[pl.ds(pl.multiple_of(t * 4, 4), 4), :]
        return carry

    lax.fori_loop(0, edges, gather, 0, unroll=8)

    def cols(c):
        return slice(c * 128, (c + 1) * 128)

    def head(c):
        return hlin[pl.ds(c, edges, stride=4), :]

    def tail(c):
        return tlin[pl.ds(c, edges, stride=4), :]

    score = jnp.zeros((edges, 128), F32)
    for a in range(2):
        b = a + 2
        hr, hi, tr, ti = head(a), head(b), tail(a), tail(b)
        rr, ri = rel_ref[:, cols(a)], rel_ref[:, cols(b)]
        qr = hr * rr - hi * ri
        qi = hr * ri + hi * rr
        ur = rr * tr + ri * ti
        ui = rr * ti - ri * tr
        score = score + (qr * tr + qi * ti)
        qf[:, cols(a)] = qr
        qf[:, cols(b)] = qi
        rhs[0:edges, cols(a)] = qr.astype(BF16)
        rhs[0:edges, cols(b)] = qi.astype(BF16)
        rhs[edges:2 * edges, cols(a)] = ur.astype(BF16)
        rhs[edges:2 * edges, cols(b)] = ui.astype(BF16)
    positive = jnp.sum(score, axis=1, keepdims=True)
    slope = 0.5 * jnp.tanh(0.5 * positive) - 0.5

    half = slots // 2
    for side in range(2):
        mine = rhs[side * edges:(side + 1) * edges, :]
        for m in range(2):
            rows = slice(m * half, (m + 1) * half)
            st = lax.dot_general(wb[rows, :], mine, NT, preferred_element_type=F32)
            weight = cnt[1 - side, rows, :]
            weight = jnp.concatenate([weight] * (edges // 128), axis=1)
            lhs[rows, side * edges:(side + 1) * edges] = (weight * jnp.tanh(0.5 * st) + weight).astype(BF16)
        dneg[side] = jnp.dot(wbt[...], lhs[:, side * edges:(side + 1) * edges], preferred_element_type=F32)

    row = lax.broadcasted_iota(jnp.int32, (slots, edges), 0)
    lhs[:, 2 * edges:3 * edges] = (row == src_v[0]).astype(F32).astype(BF16)
    lhs[:, 3 * edges:4 * edges] = (row == tgt_v[0]).astype(F32).astype(BF16)

    def put(at, c, value):
        top = value.astype(BF16)
        rhs[(2 + at) * edges:(3 + at) * edges, cols(c)] = top
        rlo[at * edges:(at + 1) * edges, cols(c)] = (value - top.astype(F32)).astype(BF16)

    for a in range(2):
        b = a + 2
        rr, ri = rel_ref[:, cols(a)], rel_ref[:, cols(b)]
        dqr = slope * tail(a) + dneg[0, cols(a), :].T
        dqi = slope * tail(b) + dneg[0, cols(b), :].T
        put(0, a, dqr * rr + dqi * ri)
        put(0, b, dqi * rr - dqr * ri)
        dur = dneg[1, cols(a), :].T
        dui = dneg[1, cols(b), :].T
        put(1, a, slope * qf[:, cols(a)] + (dur * rr - dui * ri))
        put(1, b, slope * qf[:, cols(b)] + (dur * ri + dui * rr))

    for m in range(2):
        rows = slice(m * half, (m + 1) * half)
        acc[rows, :] += (
            jnp.dot(lhs[rows, :], rhs[...], preferred_element_type=F32)
            + jnp.dot(lhs[rows, 2 * edges:], rlo[...], preferred_element_type=F32)
        )

    @pl.when(step == pl.num_programs(0) - 1)
    def _():
        hub_out[...] = acc[0:hub, :]
        for c in range(4):
            far_out[pl.ds(c, slots - hub, stride=4), :] = acc[hub:, cols(c)]


def train(w_lin, rel_rows, source, target, negative, hub, edges=256):
    buckets, count = source.shape
    negs = negative.shape[2]
    slots = w_lin.shape[0] // 4
    width = rel_rows.shape[1]
    tiles = count // edges
    steps = buckets * tiles
    whole = lambda shape: pl.BlockSpec(shape, lambda i, *_: (0,) * len(shape))
    lane = pl.BlockSpec((1, 1, edges), lambda i, *_: (i, 0, 0))
    return pl.pallas_call(
        functools.partial(train_kernel, tiles),
        grid_spec=pltpu.PrefetchScalarGridSpec(
            num_scalar_prefetch=2,
            grid=(steps,),
            in_specs=[
                whole(w_lin.shape),
                pl.BlockSpec((edges, width), lambda i, *_: (i, 0)),
                lane,
                lane,
                pl.BlockSpec((1, 2, negs), lambda i, *_: (i // tiles, 0, 0)),
            ],
            out_specs=[whole((hub, width)), whole(((slots - hub) * 4, 128))],
            scratch_shapes=[
                pltpu.VMEM((slots, width), BF16),
                pltpu.VMEM((width, slots), BF16),
                pltpu.VMEM((2, slots, 128), F32),
                pltpu.VMEM((slots, width), F32),
                pltpu.VMEM((edges * 4, 128), F32),
                pltpu.VMEM((edges * 4, 128), F32),
                pltpu.VMEM((edges, width), F32),
                pltpu.VMEM((4 * edges, width), BF16),
                pltpu.VMEM((slots, 4 * edges), BF16),
                pltpu.VMEM((2 * edges, width), BF16),
                pltpu.VMEM((2, width, edges), F32),
            ],
        ),
        out_shape=[
            jax.ShapeDtypeStruct((hub, width), F32),
            jax.ShapeDtypeStruct(((slots - hub) * 4, 128), F32),
        ],
        compiler_params=pltpu.CompilerParams(vmem_limit_bytes=56 * 1024 * 1024),
        name="train",
    )(
        source.reshape(-1), target.reshape(-1), w_lin, rel_rows,
        source.reshape(steps, 1, edges), target.reshape(steps, 1, edges), negative,
    )


MESH = pl.DeviceIdType.MESH


def ring(at, by, size):
    return lax.rem(at + by, size)


def greet(doms, works):
    dom, work = lax.axis_index("dom"), lax.axis_index("work")
    barrier = pltpu.get_barrier_semaphore()

    def call(i, carry):
        peer = (ring(dom, i // works, doms), ring(work, lax.rem(i, works), works))
        pl.semaphore_signal(barrier, inc=1, device_id=peer, device_id_type=MESH)
        return carry

    lax.fori_loop(1, doms * works, call, 0)
    pl.semaphore_wait(barrier, doms * works - 1)


def arrived(ref, sem):
    pltpu.make_async_copy(ref, ref, sem).wait()


def fetch_kernel(doms, works, cap, ent_ref, req_ref, hub_ref, ids_ref, rel_hbm,
                 w_ref, want_ref, rel_ref,
                 elin, erow, hub1, piece, send, want_s, relv,
                 rel_sem, req_send, req_recv, loc_sem, h1_send, h1_recv, h2_send, h2_recv,
                 x_send, x_recv, far_send, far_recv):
    dom, work = lax.axis_index("dom"), lax.axis_index("work")
    me = dom * works + work
    core, line = lax.rem(work, 2), work // 2
    lines = works // 2
    count = doms * works
    own = ent_ref.shape[0]
    part = own // doms * 4
    hub = works * own
    msg = cap * 4

    load = pltpu.make_async_copy(rel_hbm, relv, rel_sem)
    load.start()
    for c in range(4):
        elin[pl.ds(c, own, stride=4), :] = ent_ref[:, c * 128:(c + 1) * 128]
        erow[:, c, :] = ent_ref[:, c * 128:(c + 1) * 128]
    greet(doms, works)

    want_ref[me] = req_ref[me]

    def ask(i, carry):
        pd, pw = ring(dom, i // works, doms), ring(work, lax.rem(i, works), works)
        pltpu.make_async_remote_copy(
            src_ref=req_ref.at[pd * works + pw], dst_ref=want_ref.at[me],
            send_sem=req_send, recv_sem=req_recv, device_id=(pd, pw), device_id_type=MESH,
        ).start()
        return carry

    lax.fori_loop(1, count, ask, 0)

    hub1[dom] = elin[pl.ds(pl.multiple_of(dom * part, part), part), :]

    def spread(i, carry):
        pd = ring(dom, i, doms)
        pltpu.make_async_remote_copy(
            src_ref=elin.at[pl.ds(pl.multiple_of(pd * part, part), part), :], dst_ref=hub1.at[dom],
            send_sem=h1_send, recv_sem=h1_recv, device_id=(pd, work), device_id_type=MESH,
        ).start()
        return carry

    lax.fori_loop(1, doms, spread, 0)
    arrived(hub1.at[pl.ds(0, doms - 1)], h1_recv)
    piece[...] = hub1[hub_ref[0]]

    def rows_of(w, d):
        return w_ref.at[pl.ds(pl.multiple_of((w * doms + d) * part, part), part), :]

    pltpu.make_async_copy(piece, rows_of(work, dom), h2_recv.at[line]).start()

    def gather(i, carry):
        pd, pw = ring(dom, i // lines, doms), ring(line, lax.rem(i, lines), lines) * 2 + core
        pltpu.make_async_remote_copy(
            src_ref=piece, dst_ref=rows_of(work, dom),
            send_sem=h2_send, recv_sem=h2_recv.at[line], device_id=(pd, pw), device_id_type=MESH,
        ).start()
        return carry

    lax.fori_loop(1, doms * lines, gather, 0)

    arrived(want_ref.at[pl.ds(0, count - 1)], req_recv)
    copy = pltpu.make_async_copy(want_ref, want_s, loc_sem)
    copy.start()
    copy.wait()

    def fill(p):
        for c in range(cap):
            send[p, c * 4:(c + 1) * 4, :] = erow[want_s[p, 0, c]]

    def far_rows(p):
        return w_ref.at[pl.ds(pl.multiple_of(hub * 4 + p * msg, msg), msg), :]

    fill(me)
    pltpu.make_async_copy(send.at[me], far_rows(me), far_recv).start()

    def answer(i, carry):
        pd, pw = ring(dom, i // works, doms), ring(work, lax.rem(i, works), works)
        p = pd * works + pw
        fill(p)
        pltpu.make_async_remote_copy(
            src_ref=send.at[p], dst_ref=far_rows(me),
            send_sem=far_send, recv_sem=far_recv, device_id=(pd, pw), device_id_type=MESH,
        ).start()
        return carry

    lax.fori_loop(1, count, answer, 0)

    load.wait()

    def pick(e, carry):
        rel_ref[e] = relv[ids_ref[e]]
        return carry

    lax.fori_loop(0, rel_ref.shape[0], pick, 0, unroll=8)

    def block(w):
        return w_ref.at[pl.ds(pl.multiple_of(w * doms * part, doms * part), doms * part), :]

    def across(y, carry):
        mine = block(y * 2 + core)
        arrived(mine, h2_recv.at[y])
        pltpu.make_async_remote_copy(
            src_ref=mine, dst_ref=mine, send_sem=x_send, recv_sem=x_recv,
            device_id=(dom, line * 2 + 1 - core), device_id_type=MESH,
        ).start()
        return carry

    lax.fori_loop(0, lines, across, 0)
    half = w_ref.at[pl.ds(0, hub * 2), :]
    arrived(half, x_recv)
    arrived(w_ref.at[pl.ds(hub * 4, count * msg), :], far_recv)
    arrived(half, x_send)
    arrived(w_ref.at[pl.ds(0, (doms * lines - 1) * part), :], h2_send)
    arrived(hub1.at[pl.ds(0, doms - 1)], h1_send)
    arrived(send.at[pl.ds(0, count - 1)], far_send)
    arrived(req_ref.at[pl.ds(0, count - 1)], req_send)


def fetch(doms, works, entity_rows, asked, hub_part, relation_ids, relations):
    own, width = entity_rows.shape
    count = doms * works
    cap = 4
    slots = works * own + count * cap
    edges = relation_ids.shape[0]
    vmem, smem = pl.BlockSpec(memory_space=pltpu.VMEM), pl.BlockSpec(memory_space=pltpu.SMEM)
    dma = pltpu.SemaphoreType.DMA
    return pl.pallas_call(
        functools.partial(fetch_kernel, doms, works, cap),
        in_specs=[vmem, vmem, smem, smem, pl.BlockSpec(memory_space=pl.ANY)],
        out_specs=[vmem, vmem, vmem],
        out_shape=[
            jax.ShapeDtypeStruct((slots * 4, 128), F32),
            jax.ShapeDtypeStruct(asked.shape, jnp.int32),
            jax.ShapeDtypeStruct((edges, width), F32),
        ],
        scratch_shapes=[
            pltpu.VMEM((own * 4, 128), F32),
            pltpu.VMEM((own, 4, 128), F32),
            pltpu.VMEM((doms, own // doms * 4, 128), F32),
            pltpu.VMEM((own // doms * 4, 128), F32),
            pltpu.VMEM((count, cap * 4, 128), F32),
            pltpu.SMEM(asked.shape, jnp.int32),
            pltpu.VMEM(relations.shape, F32),
            dma, dma, dma, dma, dma, dma, dma, dma((works // 2,)), dma, dma, dma, dma,
        ],
        compiler_params=pltpu.CompilerParams(
            collective_id=0, has_side_effects=True, vmem_limit_bytes=48 * 1024 * 1024
        ),
        name="fetch",
    )(entity_rows, asked, hub_part, relation_ids, relations)


def return_kernel(doms, works, cap, hub_ref, far_ref, want_ref, part_ref, ent_ref, state_ref,
                  rows_out, state_out,
                  back, xbuf, part_buf, r2, total, r3,
                  x_send, x_recv, far_send, far_recv, r2_send, r2_recv, r3_send, r3_recv):
    dom, work = lax.axis_index("dom"), lax.axis_index("work")
    me = dom * works + work
    core, line = lax.rem(work, 2), work // 2
    lines = works // 2
    count = doms * works
    own, width = ent_ref.shape
    part = own // doms
    msg = cap * 4
    greet(doms, works)

    def swap(y, carry):
        start = pl.multiple_of((y * 2 + 1 - core) * own, own)
        pltpu.make_async_remote_copy(
            src_ref=hub_ref.at[pl.ds(start, own), :], dst_ref=xbuf.at[y],
            send_sem=x_send, recv_sem=x_recv.at[y],
            device_id=(dom, line * 2 + 1 - core), device_id_type=MESH,
        ).start()
        return carry

    lax.fori_loop(0, lines, swap, 0)

    def far_rows(p):
        return far_ref.at[pl.ds(pl.multiple_of(p * msg, msg), msg), :]

    pltpu.make_async_copy(far_rows(me), back.at[me], far_recv).start()

    def give(i, carry):
        pd, pw = ring(dom, i // works, doms), ring(work, lax.rem(i, works), works)
        pltpu.make_async_remote_copy(
            src_ref=far_rows(pd * works + pw), dst_ref=back.at[me],
            send_sem=far_send, recv_sem=far_recv, device_id=(pd, pw), device_id_type=MESH,
        ).start()
        return carry

    lax.fori_loop(1, count, give, 0)

    def add_pair(y, carry):
        arrived(xbuf.at[y], x_recv.at[y])
        start = pl.multiple_of((y * 2 + core) * own, own)
        part_buf[y] = hub_ref[pl.ds(start, own), :] + xbuf[y]
        return carry

    lax.fori_loop(0, lines, add_pair, 0)

    def piece(y, d):
        return part_buf.at[y, pl.ds(pl.multiple_of(d * part, part), part), :]

    slot = dom * lines + line
    pltpu.make_async_copy(piece(line, dom), r2.at[slot], r2_recv).start()

    def scatter(i, carry):
        pd, py = ring(dom, i // lines, doms), ring(line, lax.rem(i, lines), lines)
        pltpu.make_async_remote_copy(
            src_ref=piece(py, pd), dst_ref=r2.at[slot],
            send_sem=r2_send, recv_sem=r2_recv, device_id=(pd, py * 2 + core), device_id_type=MESH,
        ).start()
        return carry

    lax.fori_loop(1, doms * lines, scatter, 0)
    arrived(r2, r2_recv)
    total[...] = jnp.sum(r2[...], axis=0)

    pltpu.make_async_copy(total, r3.at[dom], r3_recv).start()

    def hand(i, carry):
        pltpu.make_async_remote_copy(
            src_ref=total, dst_ref=r3.at[dom],
            send_sem=r3_send, recv_sem=r3_recv, device_id=(ring(dom, i, doms), work), device_id_type=MESH,
        ).start()
        return carry

    lax.fori_loop(1, doms, hand, 0)

    arrived(back, far_recv)
    wanted = want_ref[:, 0, :].T
    row = lax.broadcasted_iota(jnp.int32, (own, count), 0)
    flat = back.reshape(count * msg, 128)
    sums = [jnp.zeros((own, 128), F32) for _ in range(4)]
    for c in range(cap):
        hot = (row == wanted[c:c + 1, :]).astype(F32)
        for k in range(4):
            got = flat[pl.ds(c * 4 + k, count, stride=msg), :]
            sums[k] += jnp.dot(hot, got, preferred_element_type=F32, precision=lax.Precision.HIGHEST)

    arrived(r3, r3_recv)
    owner = dom == part_ref[0]
    hub_sum = r3[...].reshape(own, width)
    grads = [s + jnp.where(owner, hub_sum[:, k * 128:(k + 1) * 128], 0.0) for k, s in enumerate(sums)]
    square = sum(g * g for g in grads)
    mean = jnp.sum(square, axis=1, keepdims=True) * (1.0 / width)
    old = jnp.broadcast_to(state_ref[...], (128, own)).T
    new = old + mean
    scale = 0.1 / (jnp.sqrt(new) + 1e-10)
    for k, g in enumerate(grads):
        rows_out[:, k * 128:(k + 1) * 128] = ent_ref[:, k * 128:(k + 1) * 128] - g * scale
    state_out[...] = new.T[0:1, :]

    arrived(xbuf, x_send)
    arrived(back.at[pl.ds(0, count - 1)], far_send)
    arrived(r2.at[pl.ds(0, doms * lines - 1)], r2_send)
    arrived(r3.at[pl.ds(0, doms - 1)], r3_send)


def give_back(doms, works, hub_grad, far_grad, wanted, hub_part, entity_rows, state):
    own, width = entity_rows.shape
    count = doms * works
    cap = 4
    lines = works // 2
    part = own // doms
    vmem, smem = pl.BlockSpec(memory_space=pltpu.VMEM), pl.BlockSpec(memory_space=pltpu.SMEM)
    dma = pltpu.SemaphoreType.DMA
    return pl.pallas_call(
        functools.partial(return_kernel, doms, works, cap),
        in_specs=[vmem, vmem, vmem, smem, vmem, vmem],
        out_specs=[vmem, vmem],
        out_shape=[
            jax.ShapeDtypeStruct((own, width), F32),
            jax.ShapeDtypeStruct((1, own), F32),
        ],
        scratch_shapes=[
            pltpu.VMEM((count, cap * 4, 128), F32),
            pltpu.VMEM((lines, own, width), F32),
            pltpu.VMEM((lines, own, width), F32),
            pltpu.VMEM((doms * lines, part, width), F32),
            pltpu.VMEM((part, width), F32),
            pltpu.VMEM((doms, part, width), F32),
            dma, dma((lines,)), dma, dma, dma, dma, dma, dma,
        ],
        compiler_params=pltpu.CompilerParams(
            collective_id=1, has_side_effects=True, vmem_limit_bytes=48 * 1024 * 1024
        ),
        name="give_back",
    )(hub_grad, far_grad, wanted, hub_part, entity_rows, state)


def per_device(doms, works, entity_rows, adagrad_state, relations, hub_part, requests,
               source_slot, relation_ids, target_slot, negative_slot):
    own = entity_rows.shape[0]
    count = doms * works
    asked = requests.reshape(count, 1, -1)
    asked = jnp.pad(asked, ((0, 0), (0, 0), (0, 128 - asked.shape[2])))
    w_lin, wanted, rel_rows = fetch(
        doms, works, entity_rows, asked, hub_part, relation_ids.reshape(-1), relations
    )
    hub_grad, far_grad = train(w_lin, rel_rows, source_slot, target_slot, negative_slot, works * own)
    new_rows, new_state = give_back(
        doms, works, hub_grad, far_grad, wanted, hub_part, entity_rows, adagrad_state.reshape(1, own)
    )
    return new_rows, new_state.reshape(own)


def solution(mesh):
    doms, works = mesh.shape["dom"], mesh.shape["work"]
    both = ("dom", "work")
    return jax.shard_map(
        functools.partial(per_device, doms, works),
        mesh=mesh,
        in_specs=(
            P(both, None), P(both), P(), P(), P(both, None), P(both, None),
            P(both, None), P(both, None), P(both, None, None),
        ),
        out_specs=(P(both, None), P(both)),
        check_vma=False,
    )
```

```python
import functools
import jax
import jax.numpy as jnp
from jax import lax
from jax.experimental import pallas as pl
from jax.experimental.pallas import tpu as pltpu
from jax.sharding import PartitionSpec as P

F32 = jnp.float32
BF16 = jnp.bfloat16
NT = (((1,), (1,)), ((), ()))
MESH = pl.DeviceIdType.MESH
MIB = 1024 * 1024
CAP = 4
SIDE = 4


def ring(at, by, size):
    return lax.rem(at + by, size)


def for_peers(dom, work, doms, works, act, first=0, last=None):
    near = [ring(work, k, works) for k in range(works)]
    if first == 0:
        for pw in near[1:]:
            act(dom, pw)

    def along(i, carry):
        pd = ring(dom, i, doms)
        for pw in near:
            act(pd, pw)
        return carry

    lax.fori_loop(max(first, 1), last or doms, along, 0)


def greet(doms, works):
    dom, work = lax.axis_index("dom"), lax.axis_index("work")
    barrier = pltpu.get_barrier_semaphore()

    def call(pd, pw):
        pl.semaphore_signal(barrier, inc=1, device_id=(pd, pw), device_id_type=MESH)

    for_peers(dom, work, doms, works, call)


def greeted(doms, works):
    pl.semaphore_wait(pltpu.get_barrier_semaphore(), doms * works - 1)


def arrived(ref, sem):
    pltpu.make_async_copy(ref, ref, sem).wait()


def send(src, dst, sent, landed, device):
    pltpu.make_async_remote_copy(
        src_ref=src, dst_ref=dst, send_sem=sent, recv_sem=landed, device_id=device, device_id_type=MESH
    ).start()


def cols(c):
    return slice(c * 128, (c + 1) * 128)


def fetch_kernel(doms, works, ent_ref, req_ref, hub_ref, ids_ref, rel_hbm,
                 w_ref, want_ref, rel_ref,
                 erow, hub1, piece, out_buf, reqv, want_s, relv,
                 rel_sem, req_send, req_recv, loc_sem, h1_send, h1_recv, h2_send, h2_recv,
                 x_send, x_recv, far_send, far_recv):
    dom, work = lax.axis_index("dom"), lax.axis_index("work")
    me = dom * works + work
    core, line = lax.rem(work, 2), work // 2
    z, x = dom // SIDE, lax.rem(dom, SIDE)
    lines = works // 2
    count = doms * works
    own = ent_ref.shape[0]
    half = own // 2
    part = half // doms
    hub = works * own
    per_row = 128 // CAP

    load = pltpu.make_async_copy(rel_hbm, relv, rel_sem)
    load.start()
    greet(doms, works)
    for c in range(4):
        erow[:, c, :] = ent_ref[:, cols(c)]
    for j in range(count // per_row):
        reqv[j] = req_ref[:, cols(j)]
    greeted(doms, works)

    for s in range(2):
        hub1[s, dom] = erow[pl.ds(s * half + dom * part, part)]

    def spread(i, carry):
        pd = ring(dom, i, doms)
        for s in range(2):
            send(erow.at[pl.ds(s * half + pd * part, part)], hub1.at[s, dom], h1_send, h1_recv, (pd, work))
        return carry

    lax.fori_loop(1, doms, spread, 0)

    want_ref[me] = reqv[me // per_row]

    def ask(pd, pw):
        send(reqv.at[(pd * works + pw) // per_row], want_ref.at[me], req_send, req_recv, (pd, pw))

    for_peers(dom, work, doms, works, ask)
    arrived(hub1.at[:, pl.ds(0, doms - 1)], h1_recv)

    def rows(s, y, d, n):
        return w_ref.at[pl.ds((y * 2 + core) * own + s * half + d * part, n * part)]

    at = hub_ref[0]
    for s in range(2):
        piece[s] = hub1[s, at]
    for s in range(2):
        copy = pltpu.make_async_copy(piece.at[s], rows(s, line, dom, 1), loc_sem)
        copy.start()
        copy.wait()

    def along_x(k):
        return (z * SIDE + ring(x, k, SIDE), work)

    def along_z(k):
        return (ring(z, k, SIDE) * SIDE + x, work)

    def along_y(k):
        return (dom, ring(line, k, lines) * 2 + core)

    around = (1, SIDE - 1, 2)

    def hop(refs, s, step, to):
        for k in around:
            for ref in refs:
                send(ref, ref, h2_send, h2_recv.at[s, step], to(k))

    def landed(s, step, n):
        arrived(w_ref.at[pl.ds(0, (SIDE - 1) * n * part)], h2_recv.at[s, step])

    hop([rows(0, line, dom, 1)], 0, 0, along_x)
    hop([rows(1, line, dom, 1)], 1, 0, along_y)

    arrived(want_ref.at[pl.ds(0, count - 1)], req_recv)
    copy = pltpu.make_async_copy(want_ref, want_s, loc_sem)
    copy.start()
    copy.wait()
    lane = lax.rem(me, per_row) * CAP

    def fill(p):
        for c in range(CAP):
            out_buf[p, c] = erow[want_s[p, 0, lane + c]]

    def far_rows(p):
        return w_ref.at[pl.ds(hub + p * CAP, CAP)]

    fill(me)
    pltpu.make_async_copy(out_buf.at[me], far_rows(me), far_recv).start()

    def answer(pd, pw):
        p = pd * works + pw
        fill(p)
        send(out_buf.at[p], far_rows(me), far_send, far_recv, (pd, pw))

    cuts = [0, 1, doms // 4, doms]
    for_peers(dom, work, doms, works, answer, cuts[0], cuts[1])
    landed(0, 0, 1)
    hop([rows(0, line, z * SIDE, SIDE)], 0, 1, along_z)
    landed(1, 0, 1)
    hop([rows(1, y, dom, 1) for y in range(lines)], 1, 1, along_x)
    for_peers(dom, work, doms, works, answer, cuts[1], cuts[2])
    landed(0, 1, SIDE)
    hop([rows(0, line, 0, doms)], 0, 2, along_y)
    landed(1, 1, lines)
    hop([rows(1, y, z * SIDE, SIDE) for y in range(lines)], 1, 2, along_z)
    for_peers(dom, work, doms, works, answer, cuts[2], cuts[3])

    landed(0, 2, doms)
    landed(1, 2, lines * SIDE)
    for y in range(lines):
        mine = w_ref.at[pl.ds((y * 2 + core) * own, own)]
        send(mine, mine, x_send, x_recv, (dom, line * 2 + 1 - core))
    load.wait()

    buckets, edges = ids_ref.shape
    for b in range(buckets):
        def pick(e, carry, b=b):
            rel_ref[b * edges + e] = relv[ids_ref[b, e]]
            return carry

        lax.fori_loop(0, edges, pick, 0, unroll=8)

    swapped = w_ref.at[pl.ds(0, hub // 2)]
    arrived(swapped, x_recv)
    arrived(w_ref.at[pl.ds(hub, count * CAP)], far_recv)
    arrived(swapped, x_send)
    arrived(w_ref.at[pl.ds(0, 2 * (doms * lines - 1) * part)], h2_send)
    arrived(hub1.at[:, pl.ds(0, doms - 1)], h1_send)
    arrived(out_buf.at[pl.ds(0, count - 1)], far_send)
    arrived(want_ref.at[pl.ds(0, count - 1)], req_send)


def fetch(doms, works, entity_rows, requests, hub_part, relation_ids, relations):
    own, width = entity_rows.shape
    count = doms * works
    part = own // 2 // doms
    vmem, smem = pl.BlockSpec(memory_space=pltpu.VMEM), pl.BlockSpec(memory_space=pltpu.SMEM)
    dma = pltpu.SemaphoreType.DMA
    return pl.pallas_call(
        functools.partial(fetch_kernel, doms, works),
        in_specs=[vmem, vmem, smem, smem, pl.BlockSpec(memory_space=pl.ANY)],
        out_specs=[vmem, vmem, vmem],
        out_shape=[
            jax.ShapeDtypeStruct((works * own + count * CAP, 4, 128), F32),
            jax.ShapeDtypeStruct((count, 1, 128), jnp.int32),
            jax.ShapeDtypeStruct((relation_ids.size, width), F32),
        ],
        scratch_shapes=[
            pltpu.VMEM((own, 4, 128), F32),
            pltpu.VMEM((2, doms, part, 4, 128), F32),
            pltpu.VMEM((2, part, 4, 128), F32),
            pltpu.VMEM((count, CAP, 4, 128), F32),
            pltpu.VMEM((count * CAP // 128, 1, 128), jnp.int32),
            pltpu.SMEM((count, 1, 128), jnp.int32),
            pltpu.VMEM(relations.shape, F32),
            dma, dma, dma, dma, dma, dma, dma, dma((2, 3)), dma, dma, dma, dma,
        ],
        compiler_params=pltpu.CompilerParams(
            collective_id=0, has_side_effects=True, vmem_limit_bytes=48 * MIB
        ),
        name="fetch",
    )(entity_rows, requests, hub_part, relation_ids, relations)


def train_kernel(doms, works, src_s, tgt_s, part_ref, w_ref, rel_ref, src_v, tgt_v, neg_ref, want_ref,
                 ent_ref, state_ref, rows_out, state_out,
                 wb, wbt, cnt, slot_v, gt, rneg, rhi, rlo, hlin, tlin, qf, slope_v, dneg,
                 acc, far_lin, theirs, mine, back, xbuf, r2, total, r3, want_t,
                 x_send, x_recv, far_send, far_recv, r2_send, r2_recv, r3_send, r3_recv):
    dom, work = lax.axis_index("dom"), lax.axis_index("work")
    me = dom * works + work
    core, line = lax.rem(work, 2), work // 2
    lines = works // 2
    count = doms * works
    own, width = ent_ref.shape
    hub = works * own
    slots = wb.shape[0]
    buckets, _, negs = neg_ref.shape
    edges = slot_v.shape[2]
    tiles = src_v.shape[1] // edges
    steps = buckets * tiles
    part = own // doms
    msg = CAP * 4
    greet(doms, works)

    for c in range(4):
        column = w_ref[:, c, :]
        wb[:, cols(c)] = column.astype(BF16)
        wbt[cols(c), :] = column.T.astype(BF16)
    for i in range(steps):
        spot = slice(i % tiles * edges, (i % tiles + 1) * edges)
        slot_v[2 * i] = src_v[i // tiles:i // tiles + 1, spot]
        slot_v[2 * i + 1] = tgt_v[i // tiles:i // tiles + 1, spot]

    high = lax.broadcasted_iota(jnp.int32, (16, negs), 0)
    low = lax.broadcasted_iota(jnp.int32, (128, negs), 0)
    for b in range(buckets):
        for side in range(2):
            slot = neg_ref[b, side:side + 1, :]
            top = (high == lax.shift_right_logical(slot, 7)).astype(F32).astype(BF16)
            end = (low == jnp.bitwise_and(slot, 127)).astype(F32).astype(BF16)
            table = lax.dot_general(end, top, NT, preferred_element_type=F32) * (0.5 / negs)
            for g in range(slots // 128):
                cnt[b * 2 + side, cols(g), :] = jnp.broadcast_to(table[:, g:g + 1], (128, 128))

    block = 128

    def step(i, carry):
        b, first = i // tiles, lax.rem(i, tiles) * edges
        base = i * edges

        def gather(e, carry):
            at = pl.ds(pl.multiple_of(e * 4, 4), 4)
            hlin[at, :] = w_ref[src_s[b, first + e]]
            tlin[at, :] = w_ref[tgt_s[b, first + e]]
            return carry

        lax.fori_loop(0, edges, gather, 0, unroll=8)

        def forward(k, carry):
            row = pl.multiple_of(k * block, block)
            here = pl.ds(row, block)
            there = pl.ds(pl.multiple_of(base + row, block), block)
            query = pl.ds(pl.multiple_of(2 * base + row, block), block)
            mirror = pl.ds(pl.multiple_of(2 * base + edges + row, block), block)
            score = jnp.zeros((block, 128), F32)
            for p in range(2):
                q = p + 2
                hr, hi = (hlin[pl.ds(4 * row + c, block, stride=4), :] for c in (p, q))
                tr, ti = (tlin[pl.ds(4 * row + c, block, stride=4), :] for c in (p, q))
                rr, ri = rel_ref[there, cols(p)], rel_ref[there, cols(q)]
                qr = hr * rr - hi * ri
                qi = hr * ri + hi * rr
                score = score + (qr * tr + qi * ti)
                qf[here, cols(p)] = qr
                qf[here, cols(q)] = qi
                rneg[query, cols(p)] = qr.astype(BF16)
                rneg[query, cols(q)] = qi.astype(BF16)
                rneg[mirror, cols(p)] = (rr * tr + ri * ti).astype(BF16)
                rneg[mirror, cols(q)] = (rr * ti - ri * tr).astype(BF16)
            positive = jnp.sum(score, axis=1, keepdims=True)
            slope_v[here, :] = jnp.broadcast_to(0.5 * jnp.tanh(0.5 * positive) - 0.5, (block, 128))
            return carry

        lax.fori_loop(0, edges // block, forward, 0)

        for side in range(2):
            there = pl.ds(pl.multiple_of(2 * base + side * edges, edges), edges)
            for m in range(slots // 512):
                rows = slice(m * 512, (m + 1) * 512)
                st = lax.dot_general(wb[rows, :], rneg[there, :], NT, preferred_element_type=F32)
                weight = cnt[b * 2 + 1 - side, rows, :]
                weight = jnp.concatenate([weight] * (edges // 128), axis=1)
                gt[rows, there] = (weight * jnp.tanh(0.5 * st) + weight).astype(BF16)
            dneg[side] = jnp.dot(wbt[...], gt[:, there], preferred_element_type=F32)

        def backward(k, carry):
            row = pl.multiple_of(k * block, block)
            here = pl.ds(row, block)
            there = pl.ds(pl.multiple_of(base + row, block), block)
            source = pl.ds(pl.multiple_of(2 * base + row, block), block)
            target = pl.ds(pl.multiple_of(2 * base + edges + row, block), block)

            def put(at, c, value):
                top = value.astype(BF16)
                rhi[at, cols(c)] = top
                rlo[at, cols(c)] = (value - top.astype(F32)).astype(BF16)

            slope = slope_v[here, :]
            for p in range(2):
                q = p + 2
                rr, ri = rel_ref[there, cols(p)], rel_ref[there, cols(q)]
                tr, ti = (tlin[pl.ds(4 * row + c, block, stride=4), :] for c in (p, q))
                dqr = slope * tr + dneg[0, cols(p), here].T
                dqi = slope * ti + dneg[0, cols(q), here].T
                put(source, p, dqr * rr + dqi * ri)
                put(source, q, dqi * rr - dqr * ri)
                dur = dneg[1, cols(p), here].T
                dui = dneg[1, cols(q), here].T
                put(target, p, slope * qf[here, cols(p)] + (dur * rr - dui * ri))
                put(target, q, slope * qf[here, cols(q)] + (dur * ri + dui * rr))
            return carry

        lax.fori_loop(0, edges // block, backward, 0)
        return carry

    lax.fori_loop(0, steps, step, 0)

    def gradient(starts, beside):
        acc[...] = jnp.zeros_like(acc)

        def chunk(k, carry):
            at = pl.ds(pl.multiple_of(k * edges, edges), edges)
            slot = slot_v[k]
            number = lax.broadcasted_iota(jnp.int32, (own, edges), 0)
            hot = jnp.concatenate(
                [(number == slot - start).astype(F32).astype(BF16) for start in starts], axis=0
            )
            weight = jnp.concatenate([gt[pl.ds(start, own), at] for start in starts], axis=0)
            acc[...] += (
                jnp.dot(weight, rneg[at, :], preferred_element_type=F32)
                + jnp.dot(hot, rhi[at, :], preferred_element_type=F32)
                + jnp.dot(hot, rlo[at, :], preferred_element_type=F32)
            )
            beside(k)
            return carry

        lax.fori_loop(0, 2 * steps, chunk, 0)

    gradient([hub + j * own for j in range(count * CAP // own)], lambda k: None)
    for c in range(4):
        far_lin[pl.ds(c, count * CAP, stride=4), :] = acc[:, cols(c)]
    greeted(doms, works)

    def far_rows(p):
        return far_lin.at[pl.ds(pl.multiple_of(p * msg, msg), msg), :]

    pltpu.make_async_copy(far_rows(me), back.at[me], far_recv).start()
    share = count // (4 * steps)

    def give(from_step):
        def some(k):
            for n in range(share):
                i = (from_step + k) * share + n

                @pl.when(i > 0)
                def _():
                    pd, pw = ring(dom, i // works, doms), ring(work, lax.rem(i, works), works)
                    send(far_rows(pd * works + pw), back.at[me], far_send, far_recv, (pd, pw))

        return some

    def starts(of):
        return [pl.multiple_of((y * 2 + of) * own, own) for y in range(lines)]

    gradient(starts(1 - core), give(0))
    theirs[...] = acc[...].reshape(lines, own, width)
    for y in range(lines):
        send(theirs.at[y], xbuf.at[y], x_send, x_recv.at[y], (dom, line * 2 + 1 - core))
    gradient(starts(core), give(2 * steps))

    for y in range(lines):
        arrived(xbuf.at[y], x_recv.at[y])
        mine[y] = acc[y * own:(y + 1) * own, :] + xbuf[y]

    def piece(y, d):
        return mine.at[y, pl.ds(pl.multiple_of(d * part, part), part), :]

    slot = dom * lines + line
    pltpu.make_async_copy(piece(line, dom), r2.at[slot], r2_recv).start()

    def scatter(i, carry):
        pd, py = ring(dom, i // lines, doms), ring(line, lax.rem(i, lines), lines)
        send(piece(py, pd), r2.at[slot], r2_send, r2_recv, (pd, py * 2 + core))
        return carry

    lax.fori_loop(1, doms * lines, scatter, 0)

    want_t[...] = want_ref[:, 0, :].T
    arrived(back, far_recv)
    lane = lax.rem(me, 128 // CAP) * CAP
    row = lax.broadcasted_iota(jnp.int32, (own, count), 0)
    flat = back.reshape(count * msg, 128)
    sums = [jnp.zeros((own, 128), F32) for _ in range(4)]
    for c in range(CAP):
        hot = (row == want_t[pl.ds(lane + c, 1), :]).astype(F32)
        for k in range(4):
            got = flat[pl.ds(c * 4 + k, count, stride=msg), :]
            sums[k] += jnp.dot(hot, got, preferred_element_type=F32, precision=lax.Precision.HIGHEST)
    for k in range(4):
        acc[0:own, cols(k)] = sums[k]

    arrived(r2, r2_recv)
    total[...] = jnp.sum(r2[...], axis=0)
    pltpu.make_async_copy(total, r3.at[dom], r3_recv).start()

    def hand(i, carry):
        send(total, r3.at[dom], r3_send, r3_recv, (ring(dom, i, doms), work))
        return carry

    lax.fori_loop(1, doms, hand, 0)
    arrived(r3, r3_recv)
    owner = dom == part_ref[0]
    hub_sum = r3[...].reshape(own, width)
    grads = [acc[0:own, cols(k)] + jnp.where(owner, hub_sum[:, cols(k)], 0.0) for k in range(4)]
    square = sum(g * g for g in grads)
    mean = jnp.sum(square, axis=1, keepdims=True) * (1.0 / width)
    old = jnp.broadcast_to(state_ref[...], (128, own)).T
    new = old + mean
    scale = 0.1 / (jnp.sqrt(new) + 1e-10)
    for k, g in enumerate(grads):
        rows_out[:, cols(k)] = ent_ref[:, cols(k)] - g * scale
    state_out[...] = new.T[0:1, :]

    arrived(xbuf, x_send)
    arrived(back.at[pl.ds(0, count - 1)], far_send)
    arrived(r2.at[pl.ds(0, doms * lines - 1)], r2_send)
    arrived(r3.at[pl.ds(0, doms - 1)], r3_send)


def train(doms, works, w_rows, rel_rows, source, target, negative, wanted, hub_part, entity_rows, state,
          edges=512):
    own, width = entity_rows.shape
    count = doms * works
    lines = works // 2
    part = own // doms
    slots = w_rows.shape[0]
    total = source.size
    vmem, smem = pl.BlockSpec(memory_space=pltpu.VMEM), pl.BlockSpec(memory_space=pltpu.SMEM)
    dma = pltpu.SemaphoreType.DMA
    return pl.pallas_call(
        functools.partial(train_kernel, doms, works),
        in_specs=[smem] * 3 + [vmem] * 8,
        out_specs=[vmem, vmem],
        out_shape=[
            jax.ShapeDtypeStruct((own, width), F32),
            jax.ShapeDtypeStruct((1, own), F32),
        ],
        scratch_shapes=[
            pltpu.VMEM((slots, width), BF16),
            pltpu.VMEM((width, slots), BF16),
            pltpu.VMEM((2 * source.shape[0], slots, 128), F32),
            pltpu.VMEM((2 * total // edges, 1, edges), jnp.int32),
            pltpu.VMEM((slots, 2 * total), BF16),
            pltpu.VMEM((2 * total, width), BF16),
            pltpu.VMEM((2 * total, width), BF16),
            pltpu.VMEM((2 * total, width), BF16),
            pltpu.VMEM((edges * 4, 128), F32),
            pltpu.VMEM((edges * 4, 128), F32),
            pltpu.VMEM((edges, width), F32),
            pltpu.VMEM((edges, 128), F32),
            pltpu.VMEM((2, width, edges), F32),
            pltpu.VMEM((lines * own, width), F32),
            pltpu.VMEM((count * CAP * 4, 128), F32),
            pltpu.VMEM((lines, own, width), F32),
            pltpu.VMEM((lines, own, width), F32),
            pltpu.VMEM((count, CAP * 4, 128), F32),
            pltpu.VMEM((lines, own, width), F32),
            pltpu.VMEM((doms * lines, part, width), F32),
            pltpu.VMEM((part, width), F32),
            pltpu.VMEM((doms, part, width), F32),
            pltpu.VMEM((128, count), jnp.int32),
            dma, dma((lines,)), dma, dma, dma, dma, dma, dma,
        ],
        compiler_params=pltpu.CompilerParams(
            collective_id=1, has_side_effects=True, vmem_limit_bytes=60 * MIB
        ),
        name="train",
    )(source, target, hub_part, w_rows, rel_rows, source, target, negative, wanted, entity_rows, state)


def per_device(doms, works, entity_rows, adagrad_state, relations, hub_part, requests,
               source_slot, relation_ids, target_slot, negative_slot):
    own = entity_rows.shape[0]
    w_rows, wanted, rel_rows = fetch(
        doms, works, entity_rows, requests, hub_part, relation_ids, relations
    )
    new_rows, new_state = train(
        doms, works, w_rows, rel_rows, source_slot, target_slot, negative_slot, wanted, hub_part,
        entity_rows, adagrad_state.reshape(1, own)
    )
    return new_rows, new_state.reshape(own)


def solution(mesh):
    doms, works = mesh.shape["dom"], mesh.shape["work"]
    both = ("dom", "work")
    return jax.shard_map(
        functools.partial(per_device, doms, works),
        mesh=mesh,
        in_specs=(
            P(both, None), P(both), P(), P(), P(both, None), P(both, None),
            P(both, None), P(both, None), P(both, None, None),
        ),
        out_specs=(P(both, None), P(both)),
        check_vma=False,
    )
```

```python
import functools
import jax
import jax.numpy as jnp
from jax import lax
from jax.experimental import pallas as pl
from jax.experimental.pallas import tpu as pltpu
from jax.sharding import PartitionSpec as P

F32 = jnp.float32
BF16 = jnp.bfloat16
NT = (((1,), (1,)), ((), ()))
MESH = pl.DeviceIdType.MESH
MIB = 1024 * 1024
CAP = 4
SIDE = 4


def ring(at, by, size):
    return lax.rem(at + by, size)


def for_peers(dom, work, doms, works, act, first=0, last=None):
    near = [ring(work, k, works) for k in range(works)]
    if first == 0:
        for pw in near[1:]:
            act(dom, pw)

    def along(i, carry):
        pd = ring(dom, i, doms)
        for pw in near:
            act(pd, pw)
        return carry

    lax.fori_loop(max(first, 1), last or doms, along, 0)


def greet(doms, works):
    dom, work = lax.axis_index("dom"), lax.axis_index("work")
    barrier = pltpu.get_barrier_semaphore()

    def call(pd, pw):
        pl.semaphore_signal(barrier, inc=1, device_id=(pd, pw), device_id_type=MESH)

    for_peers(dom, work, doms, works, call)


def greeted(doms, works):
    pl.semaphore_wait(pltpu.get_barrier_semaphore(), doms * works - 1)


def arrived(ref, sem):
    pltpu.make_async_copy(ref, ref, sem).wait()


def send(src, dst, sent, landed, device):
    pltpu.make_async_remote_copy(
        src_ref=src, dst_ref=dst, send_sem=sent, recv_sem=landed, device_id=device, device_id_type=MESH
    ).start()


def cols(c):
    return slice(c * 128, (c + 1) * 128)


def window_kernel(doms, works, edges, hub_ref, ids_ref, source_s, target_s, ent_hbm, req_hbm, rel_hbm,
                  src_hbm, tgt_hbm, neg_hbm, state_hbm,
                  rows_out, state_out,
                  ent_ref, req_ref, src_v, tgt_v, neg_ref, state_ref,
                  w_ref, want_ref, rel_ref, erow, hub1, piece, out_buf, reqv, want_s, relv,
                  wb, wbt, cnt, slot_v, gt, rneg, rhi, rlo, hlin, tlin, slope_v, dneg,
                  far_lin, back, xbuf, r2, total, r3, want_t,
                  in_sem, rel_sem, req_send, req_recv, loc_sem, h1_send, h1_recv, h2_send, h2_recv,
                  x_send, x_recv, far_send, far_recv,
                  y_send, y_recv, back_send, back_recv, r2_send, r2_recv, r3_send, r3_recv):
    dom, work = lax.axis_index("dom"), lax.axis_index("work")
    me = dom * works + work
    core, line = lax.rem(work, 2), work // 2
    z, x = dom // SIDE, lax.rem(dom, SIDE)
    lines = works // 2
    count = doms * works
    own = ent_ref.shape[0]
    half = own // 2
    part = half // doms
    hub = works * own
    per_row = 128 // CAP
    buckets, per_bucket = ids_ref.shape
    width = ent_ref.shape[1]
    slots = wb.shape[0]
    negs = neg_ref.shape[2]
    tiles = per_bucket // edges
    steps = buckets * tiles

    load = pltpu.make_async_copy(rel_hbm, relv, rel_sem)
    moves = [
        pltpu.make_async_copy(src, dst, in_sem.at[i]) for i, (src, dst) in enumerate((
            (ent_hbm, ent_ref), (req_hbm, req_ref), (src_hbm, src_v), (tgt_hbm, tgt_v), (neg_hbm, neg_ref),
            (state_hbm, state_ref),
        ))
    ]
    for move in moves:
        move.start()
    load.start()
    greet(doms, works)
    for move in moves:
        move.wait()
    for c in range(4):
        erow[:, c, :] = ent_ref[:, cols(c)]
    for j in range(count // per_row):
        reqv[j] = req_ref[:, cols(j)]
    greeted(doms, works)

    for s in range(2):
        hub1[s, dom] = erow[pl.ds(s * half + dom * part, part)]

    def spread(i, carry):
        pd = ring(dom, i, doms)
        for s in range(2):
            send(erow.at[pl.ds(s * half + pd * part, part)], hub1.at[s, dom], h1_send, h1_recv, (pd, work))
        return carry

    lax.fori_loop(1, doms, spread, 0)

    want_ref[me] = reqv[me // per_row]

    def ask(pd, pw):
        send(reqv.at[(pd * works + pw) // per_row], want_ref.at[me], req_send, req_recv, (pd, pw))

    for_peers(dom, work, doms, works, ask)
    arrived(hub1.at[:, pl.ds(0, doms - 1)], h1_recv)

    def rows(s, y, d, n):
        return w_ref.at[pl.ds((y * 2 + core) * own + s * half + d * part, n * part)]

    at = hub_ref[0]
    for s in range(2):
        piece[s] = hub1[s, at]
    for s in range(2):
        copy = pltpu.make_async_copy(piece.at[s], rows(s, line, dom, 1), loc_sem)
        copy.start()
        copy.wait()

    def along_x(k):
        return (z * SIDE + ring(x, k, SIDE), work)

    def along_z(k):
        return (ring(z, k, SIDE) * SIDE + x, work)

    def along_y(k):
        return (dom, ring(line, k, lines) * 2 + core)

    around = (1, SIDE - 1, 2)

    def hop(refs, s, step, to):
        for k in around:
            for ref in refs:
                send(ref, ref, h2_send, h2_recv.at[s, step], to(k))

    def landed(s, step, n):
        arrived(w_ref.at[pl.ds(0, (SIDE - 1) * n * part)], h2_recv.at[s, step])

    hop([rows(0, line, dom, 1)], 0, 0, along_x)
    hop([rows(1, line, dom, 1)], 1, 0, along_y)

    arrived(want_ref.at[pl.ds(0, count - 1)], req_recv)
    copy = pltpu.make_async_copy(want_ref, want_s, loc_sem)
    copy.start()
    copy.wait()
    lane = lax.rem(me, per_row) * CAP

    def fill(p):
        for c in range(CAP):
            out_buf[p, c] = erow[want_s[p, 0, lane + c]]

    def far_rows(p):
        return w_ref.at[pl.ds(hub + p * CAP, CAP)]

    fill(me)
    pltpu.make_async_copy(out_buf.at[me], far_rows(me), far_recv).start()

    def answer(pd, pw):
        p = pd * works + pw
        fill(p)
        send(out_buf.at[p], far_rows(me), far_send, far_recv, (pd, pw))

    cuts = [0, 1, doms // 4, doms]
    for_peers(dom, work, doms, works, answer, cuts[0], cuts[1])
    landed(0, 0, 1)
    hop([rows(0, line, z * SIDE, SIDE)], 0, 1, along_z)
    landed(1, 0, 1)
    hop([rows(1, y, dom, 1) for y in range(lines)], 1, 1, along_x)
    for_peers(dom, work, doms, works, answer, cuts[1], cuts[2])
    landed(0, 1, SIDE)
    hop([rows(0, line, 0, doms)], 0, 2, along_y)
    landed(1, 1, lines)
    hop([rows(1, y, z * SIDE, SIDE) for y in range(lines)], 1, 2, along_z)
    for_peers(dom, work, doms, works, answer, cuts[2], cuts[3])

    load.wait()

    def pick(b):
        def one(e, carry):
            rel_ref[b * per_bucket + e] = relv[ids_ref[b, e]]
            return carry

        lax.fori_loop(0, per_bucket, one, 0, unroll=8)

    for b in range(buckets - 1):
        pick(b)

    landed(0, 2, doms)
    landed(1, 2, lines * SIDE)
    for y in range(lines):
        mine = w_ref.at[pl.ds((y * 2 + core) * own, own)]
        send(mine, mine, x_send, x_recv, (dom, line * 2 + 1 - core))
    pick(buckets - 1)

    for i in range(steps):
        spot = slice(i % tiles * edges, (i % tiles + 1) * edges)
        slot_v[2 * i] = src_v[i // tiles:i // tiles + 1, spot]
        slot_v[2 * i + 1] = tgt_v[i // tiles:i // tiles + 1, spot]

    high = lax.broadcasted_iota(jnp.int32, (16, negs), 0)
    low = lax.broadcasted_iota(jnp.int32, (128, negs), 0)
    for b in range(buckets):
        for side in range(2):
            slot = neg_ref[b, side:side + 1, :]
            top = (high == lax.shift_right_logical(slot, 7)).astype(F32).astype(BF16)
            end = (low == jnp.bitwise_and(slot, 127)).astype(F32).astype(BF16)
            table = lax.dot_general(end, top, NT, preferred_element_type=F32) * (0.5 / negs)
            for g in range(slots // 128):
                cnt[b * 2 + side, cols(g), :] = jnp.broadcast_to(table[:, g:g + 1], (128, 128))

    swapped = w_ref.at[pl.ds(0, hub // 2)]
    arrived(swapped, x_recv)
    arrived(w_ref.at[pl.ds(hub, count * CAP)], far_recv)
    for c in range(4):
        column = w_ref[:, c, :]
        wb[:, cols(c)] = column.astype(BF16)
        wbt[cols(c), :] = column.T.astype(BF16)

    block = 128
    eighth = own // doms
    msg = CAP * 4
    acc, theirs, mine, qf = (relv.at[pl.ds(k * lines * own, lines * own), :] for k in range(4))

    def step(i, carry):
        b, first = i // tiles, lax.rem(i, tiles) * edges
        base = i * edges

        def gather(e, carry):
            at = pl.ds(pl.multiple_of(e * 4, 4), 4)
            hlin[at, :] = w_ref[source_s[b, first + e]]
            tlin[at, :] = w_ref[target_s[b, first + e]]
            return carry

        lax.fori_loop(0, edges, gather, 0, unroll=8)

        def forward(k, carry):
            row = pl.multiple_of(k * block, block)
            here = pl.ds(row, block)
            there = pl.ds(pl.multiple_of(base + row, block), block)
            query = pl.ds(pl.multiple_of(2 * base + row, block), block)
            mirror = pl.ds(pl.multiple_of(2 * base + edges + row, block), block)
            score = jnp.zeros((block, 128), F32)
            for p in range(2):
                q = p + 2
                hr, hi = (hlin[pl.ds(4 * row + c, block, stride=4), :] for c in (p, q))
                tr, ti = (tlin[pl.ds(4 * row + c, block, stride=4), :] for c in (p, q))
                rr, ri = rel_ref[there, cols(p)], rel_ref[there, cols(q)]
                qr = hr * rr - hi * ri
                qi = hr * ri + hi * rr
                score = score + (qr * tr + qi * ti)
                qf[here, cols(p)] = qr
                qf[here, cols(q)] = qi
                rneg[query, cols(p)] = qr.astype(BF16)
                rneg[query, cols(q)] = qi.astype(BF16)
                rneg[mirror, cols(p)] = (rr * tr + ri * ti).astype(BF16)
                rneg[mirror, cols(q)] = (rr * ti - ri * tr).astype(BF16)
            positive = jnp.sum(score, axis=1, keepdims=True)
            slope_v[here, :] = jnp.broadcast_to(0.5 * jnp.tanh(0.5 * positive) - 0.5, (block, 128))
            return carry

        lax.fori_loop(0, edges // block, forward, 0)

        for side in range(2):
            there = pl.ds(pl.multiple_of(2 * base + side * edges, edges), edges)
            for m in range(slots // 512):
                rows = slice(m * 512, (m + 1) * 512)
                st = lax.dot_general(wb[rows, :], rneg[there, :], NT, preferred_element_type=F32)
                weight = cnt[b * 2 + 1 - side, rows, :]
                weight = jnp.concatenate([weight] * (edges // 128), axis=1)
                gt[rows, there] = (weight * jnp.tanh(0.5 * st) + weight).astype(BF16)
            dneg[side] = jnp.dot(wbt[...], gt[:, there], preferred_element_type=F32)

        def backward(k, carry):
            row = pl.multiple_of(k * block, block)
            here = pl.ds(row, block)
            there = pl.ds(pl.multiple_of(base + row, block), block)
            source = pl.ds(pl.multiple_of(2 * base + row, block), block)
            target = pl.ds(pl.multiple_of(2 * base + edges + row, block), block)

            def put(at, c, value):
                top = value.astype(BF16)
                rhi[at, cols(c)] = top
                rlo[at, cols(c)] = (value - top.astype(F32)).astype(BF16)

            slope = slope_v[here, :]
            for p in range(2):
                q = p + 2
                rr, ri = rel_ref[there, cols(p)], rel_ref[there, cols(q)]
                tr, ti = (tlin[pl.ds(4 * row + c, block, stride=4), :] for c in (p, q))
                dqr = slope * tr + dneg[0, cols(p), here].T
                dqi = slope * ti + dneg[0, cols(q), here].T
                put(source, p, dqr * rr + dqi * ri)
                put(source, q, dqi * rr - dqr * ri)
                dur = dneg[1, cols(p), here].T
                dui = dneg[1, cols(q), here].T
                put(target, p, slope * qf[here, cols(p)] + (dur * rr - dui * ri))
                put(target, q, slope * qf[here, cols(q)] + (dur * ri + dui * rr))
            return carry

        lax.fori_loop(0, edges // block, backward, 0)
        return carry

    lax.fori_loop(0, steps, step, 0)

    def gradient(starts, beside):
        acc[...] = jnp.zeros(acc.shape, F32)

        def chunk(k, carry):
            at = pl.ds(pl.multiple_of(k * edges, edges), edges)
            slot = slot_v[k]
            number = lax.broadcasted_iota(jnp.int32, (own, edges), 0)
            hot = jnp.concatenate(
                [(number == slot - start).astype(F32).astype(BF16) for start in starts], axis=0
            )
            weight = jnp.concatenate([gt[pl.ds(start, own), at] for start in starts], axis=0)
            acc[...] += (
                jnp.dot(weight, rneg[at, :], preferred_element_type=F32)
                + jnp.dot(hot, rhi[at, :], preferred_element_type=F32)
                + jnp.dot(hot, rlo[at, :], preferred_element_type=F32)
            )
            beside(k)
            return carry

        lax.fori_loop(0, 2 * steps, chunk, 0)

    gradient([hub + j * own for j in range(count * CAP // own)], lambda k: None)
    for c in range(4):
        far_lin[pl.ds(c, count * CAP, stride=4), :] = acc[:, cols(c)]
    def far_grads(p):
        return far_lin.at[pl.ds(pl.multiple_of(p * msg, msg), msg), :]

    pltpu.make_async_copy(far_grads(me), back.at[me], back_recv).start()
    share = count // (4 * steps)

    def give(from_step):
        def some(k):
            for n in range(share):
                i = (from_step + k) * share + n

                @pl.when(i > 0)
                def _():
                    pd, pw = ring(dom, i // works, doms), ring(work, lax.rem(i, works), works)
                    send(far_grads(pd * works + pw), back.at[me], back_send, back_recv, (pd, pw))

        return some

    def starts(of):
        return [pl.multiple_of((y * 2 + of) * own, own) for y in range(lines)]

    gradient(starts(1 - core), give(0))
    theirs[...] = acc[...]
    for y in range(lines):
        send(theirs.at[pl.ds(y * own, own), :], xbuf.at[y], y_send, y_recv.at[y], (dom, line * 2 + 1 - core))
    gradient(starts(core), give(2 * steps))

    for y in range(lines):
        arrived(xbuf.at[y], y_recv.at[y])
        mine[pl.ds(y * own, own), :] = acc[pl.ds(y * own, own), :] + xbuf[y]

    def piece(y, d):
        return mine.at[pl.ds(pl.multiple_of(y * own + d * eighth, eighth), eighth), :]

    slot = dom * lines + line
    pltpu.make_async_copy(piece(line, dom), r2.at[slot], r2_recv).start()

    def scatter(i, carry):
        pd, py = ring(dom, i // lines, doms), ring(line, lax.rem(i, lines), lines)
        send(piece(py, pd), r2.at[slot], r2_send, r2_recv, (pd, py * 2 + core))
        return carry

    lax.fori_loop(1, doms * lines, scatter, 0)

    want_t[...] = want_ref[:, 0, :].T
    arrived(back, back_recv)
    row = lax.broadcasted_iota(jnp.int32, (own, count), 0)
    flat = back.reshape(count * msg, 128)
    sums = [jnp.zeros((own, 128), F32) for _ in range(4)]
    for c in range(CAP):
        hot = (row == want_t[pl.ds(lane + c, 1), :]).astype(F32)
        for k in range(4):
            got = flat[pl.ds(c * 4 + k, count, stride=msg), :]
            sums[k] += jnp.dot(hot, got, preferred_element_type=F32, precision=lax.Precision.HIGHEST)
    for k in range(4):
        acc[0:own, cols(k)] = sums[k]

    arrived(r2, r2_recv)
    total[...] = jnp.sum(r2[...], axis=0)
    pltpu.make_async_copy(total, r3.at[dom], r3_recv).start()

    def hand(i, carry):
        send(total, r3.at[dom], r3_send, r3_recv, (ring(dom, i, doms), work))
        return carry

    lax.fori_loop(1, doms, hand, 0)
    arrived(r3, r3_recv)
    owner = dom == hub_ref[0]
    hub_sum = r3[...].reshape(own, width)
    grads = [acc[0:own, cols(k)] + jnp.where(owner, hub_sum[:, cols(k)], 0.0) for k in range(4)]
    square = sum(g * g for g in grads)
    mean = jnp.sum(square, axis=1, keepdims=True) * (1.0 / width)
    old = jnp.broadcast_to(state_ref[...], (128, own)).T
    new = old + mean
    scale = 0.1 / (jnp.sqrt(new) + 1e-10)
    for k, g in enumerate(grads):
        rows_out[:, cols(k)] = ent_ref[:, cols(k)] - g * scale
    state_out[...] = new.T[0:1, :]

    arrived(xbuf, y_send)
    arrived(back.at[pl.ds(0, count - 1)], back_send)
    arrived(r2.at[pl.ds(0, doms * lines - 1)], r2_send)
    arrived(r3.at[pl.ds(0, doms - 1)], r3_send)
    arrived(swapped, x_send)
    arrived(w_ref.at[pl.ds(0, 2 * (doms * lines - 1) * part)], h2_send)
    arrived(hub1.at[:, pl.ds(0, doms - 1)], h1_send)
    arrived(out_buf.at[pl.ds(0, count - 1)], far_send)
    arrived(want_ref.at[pl.ds(0, count - 1)], req_send)


def window(doms, works, entity_rows, state, relations, hub_part, requests, source, relation_ids, target, negative,
           edges=512):
    own, width = entity_rows.shape
    count = doms * works
    lines = works // 2
    part = own // 2 // doms
    eighth = own // doms
    slots = works * own + count * CAP
    total = source.size
    any_, smem = pl.BlockSpec(memory_space=pl.ANY), pl.BlockSpec(memory_space=pltpu.SMEM)
    vmem = pl.BlockSpec(memory_space=pltpu.VMEM)
    dma = pltpu.SemaphoreType.DMA
    i32 = jnp.int32
    return pl.pallas_call(
        functools.partial(window_kernel, doms, works, edges),
        in_specs=[smem] * 4 + [any_] * 7,
        out_specs=[vmem, vmem],
        out_shape=[
            jax.ShapeDtypeStruct((own, width), F32),
            jax.ShapeDtypeStruct((1, own), F32),
        ],
        scratch_shapes=[
            pltpu.VMEM((own, width), F32),
            pltpu.VMEM(requests.shape, i32),
            pltpu.VMEM(source.shape, i32),
            pltpu.VMEM(target.shape, i32),
            pltpu.VMEM(negative.shape, i32),
            pltpu.VMEM(state.shape, F32),
            pltpu.VMEM((slots, 4, 128), F32),
            pltpu.VMEM((count, 1, 128), i32),
            pltpu.VMEM((total, width), F32),
            pltpu.VMEM((own, 4, 128), F32),
            pltpu.VMEM((2, doms, part, 4, 128), F32),
            pltpu.VMEM((2, part, 4, 128), F32),
            pltpu.VMEM((count, CAP, 4, 128), F32),
            pltpu.VMEM((count * CAP // 128, 1, 128), i32),
            pltpu.SMEM((count, 1, 128), i32),
            pltpu.VMEM(relations.shape, F32),
            pltpu.VMEM((slots, width), BF16),
            pltpu.VMEM((width, slots), BF16),
            pltpu.VMEM((2 * source.shape[0], slots, 128), F32),
            pltpu.VMEM((2 * total // edges, 1, edges), i32),
            pltpu.VMEM((slots, 2 * total), BF16),
            pltpu.VMEM((2 * total, width), BF16),
            pltpu.VMEM((2 * total, width), BF16),
            pltpu.VMEM((2 * total, width), BF16),
            pltpu.VMEM((edges * 4, 128), F32),
            pltpu.VMEM((edges * 4, 128), F32),
            pltpu.VMEM((edges, 128), F32),
            pltpu.VMEM((2, width, edges), F32),
            pltpu.VMEM((count * CAP * 4, 128), F32),
            pltpu.VMEM((count, CAP * 4, 128), F32),
            pltpu.VMEM((lines, own, width), F32),
            pltpu.VMEM((doms * lines, eighth, width), F32),
            pltpu.VMEM((eighth, width), F32),
            pltpu.VMEM((doms, eighth, width), F32),
            pltpu.VMEM((128, count), i32),
            dma((6,)), dma, dma, dma, dma, dma, dma, dma, dma((2, 3)), dma, dma, dma, dma,
            dma, dma((lines,)), dma, dma, dma, dma, dma, dma,
        ],
        compiler_params=pltpu.CompilerParams(
            collective_id=0, has_side_effects=True, vmem_limit_bytes=60 * MIB
        ),
        name="window",
    )(hub_part, relation_ids, source, target, entity_rows, requests, relations, source, target, negative, state)


def per_device(doms, works, entity_rows, adagrad_state, *others):
    own = entity_rows.shape[0]
    new_rows, new_state = window(doms, works, entity_rows, adagrad_state.reshape(1, own), *others)
    return new_rows, new_state.reshape(own)


def solution(mesh):
    doms, works = mesh.shape["dom"], mesh.shape["work"]
    both = ("dom", "work")
    return jax.shard_map(
        functools.partial(per_device, doms, works),
        mesh=mesh,
        in_specs=(
            P(both, None), P(both), P(), P(), P(both, None), P(both, None),
            P(both, None), P(both, None), P(both, None, None),
        ),
        out_specs=(P(both, None), P(both)),
        check_vma=False,
    )
```

```python
import functools
import jax
import jax.numpy as jnp
from jax import lax
from jax.experimental import pallas as pl
from jax.experimental.pallas import tpu as pltpu
from jax.sharding import PartitionSpec as P

F32 = jnp.float32
BF16 = jnp.bfloat16
F8 = jnp.float8_e4m3fn
LOW = 1024.0
NT = (((1,), (1,)), ((), ()))
MESH = pl.DeviceIdType.MESH
MIB = 1024 * 1024
CAP = 4
SIDE = 4


def ring(at, by, size):
    return lax.rem(at + by, size)


def for_peers(dom, work, doms, works, act, first=0, last=None):
    near = [ring(work, k, works) for k in range(works)]
    if first == 0:
        for pw in near[1:]:
            act(dom, pw)

    def along(i, carry):
        pd = ring(dom, i, doms)
        for pw in near:
            act(pd, pw)
        return carry

    lax.fori_loop(max(first, 1), last or doms, along, 0)


def greet(doms, works):
    dom, work = lax.axis_index("dom"), lax.axis_index("work")
    barrier = pltpu.get_barrier_semaphore()

    def call(pd, pw):
        pl.semaphore_signal(barrier, inc=1, device_id=(pd, pw), device_id_type=MESH)

    for_peers(dom, work, doms, works, call)


def greeted(doms, works):
    pl.semaphore_wait(pltpu.get_barrier_semaphore(), doms * works - 1)


def arrived(ref, sem):
    pltpu.make_async_copy(ref, ref, sem).wait()


def send(src, dst, sent, landed, device):
    pltpu.make_async_remote_copy(
        src_ref=src, dst_ref=dst, send_sem=sent, recv_sem=landed, device_id=device, device_id_type=MESH
    ).start()


def cols(c):
    return slice(c * 128, (c + 1) * 128)


def window_kernel(doms, works, edges, hub_ref, ids_ref, source_s, target_s, ent_hbm, req_hbm, rel_hbm,
                  src_hbm, tgt_hbm, neg_hbm, state_hbm,
                  rows_out, state_out,
                  ent_ref, req_ref, src_v, tgt_v, neg_ref, state_ref,
                  w_ref, want_ref, rel_ref, erow, hub1, out_buf, reqv, want_s, relv,
                  wb, wbt, cnt, slot_v, gt, rneg, rhi, rlo, hlin, tlin, slope_v, dneg,
                  far_lin, back, xbuf, r2, total, r3, want_t,
                  in_sem, rel_sem, req_send, req_recv, loc_sem, h1_send, h1_recv, h2_send, h2_recv,
                  x_send, x_recv, far_send, far_recv,
                  y_send, y_recv, back_send, back_recv, r2_send, r2_recv, r3_send, r3_recv):
    dom, work = lax.axis_index("dom"), lax.axis_index("work")
    me = dom * works + work
    core, line = lax.rem(work, 2), work // 2
    z, x = dom // SIDE, lax.rem(dom, SIDE)
    lines = works // 2
    count = doms * works
    own = ent_ref.shape[0]
    half = own // 2
    part = half // doms
    hub = works * own
    per_row = 128 // CAP
    buckets, per_bucket = ids_ref.shape
    width = ent_ref.shape[1]
    slots = wb.shape[0]
    negs = neg_ref.shape[2]
    tiles = per_bucket // edges
    steps = buckets * tiles

    load = pltpu.make_async_copy(rel_hbm, relv, rel_sem)
    moves = [
        pltpu.make_async_copy(src, dst, in_sem.at[i]) for i, (src, dst) in enumerate((
            (ent_hbm, ent_ref), (req_hbm, req_ref), (src_hbm, src_v), (tgt_hbm, tgt_v), (neg_hbm, neg_ref),
            (state_hbm, state_ref),
        ))
    ]
    for move in moves:
        move.start()
    load.start()
    greet(doms, works)
    for move in moves:
        move.wait()
    for c in range(4):
        erow[:, c, :] = ent_ref[:, cols(c)]
    for j in range(count // per_row):
        reqv[j] = req_ref[:, cols(j)]
    greeted(doms, works)

    for s in range(2):
        hub1[s, dom] = erow[pl.ds(s * half + dom * part, part)]

    def spread(i, carry):
        pd = ring(dom, i, doms)
        for s in range(2):
            send(erow.at[pl.ds(s * half + pd * part, part)], hub1.at[s, dom], h1_send, h1_recv, (pd, work))
        return carry

    lax.fori_loop(1, doms, spread, 0)

    want_ref[me] = reqv[me // per_row]

    def ask(pd, pw):
        send(reqv.at[(pd * works + pw) // per_row], want_ref.at[me], req_send, req_recv, (pd, pw))

    for_peers(dom, work, doms, works, ask)

    def rows(s, y, d, n):
        return w_ref.at[pl.ds((y * 2 + core) * own + s * half + d * part, n * part)]

    def along_x(k):
        return (z * SIDE + ring(x, k, SIDE), work)

    def along_z(k):
        return (ring(z, k, SIDE) * SIDE + x, work)

    def along_y(k):
        return (dom, ring(line, k, lines) * 2 + core)

    around = (1, SIDE - 1, 2)

    def hop(refs, s, step, to):
        for k in around:
            for ref in refs:
                send(ref, ref, h2_send, h2_recv.at[s, step], to(k))

    def landed(s, step, n):
        arrived(w_ref.at[pl.ds(0, (SIDE - 1) * n * part)], h2_recv.at[s, step])

    arrived(hub1.at[:, pl.ds(0, doms - 1)], h1_recv)
    at = hub_ref[0]
    for s in range(2):
        w_ref[pl.ds((line * 2 + core) * own + s * half + dom * part, part)] = hub1[s, at]
    hop([rows(0, line, dom, 1)], 0, 0, along_x)
    hop([rows(1, line, dom, 1)], 1, 0, along_y)

    arrived(want_ref.at[pl.ds(0, count - 1)], req_recv)
    copy = pltpu.make_async_copy(want_ref, want_s, loc_sem)
    copy.start()
    copy.wait()
    lane = lax.rem(me, per_row) * CAP

    def fill(p):
        for c in range(CAP):
            out_buf[p, c] = erow[want_s[p, 0, lane + c]]

    def far_rows(p):
        return w_ref.at[pl.ds(hub + p * CAP, CAP)]

    fill(me)
    pltpu.make_async_copy(out_buf.at[me], far_rows(me), far_recv).start()

    def answer(pd, pw):
        p = pd * works + pw
        fill(p)
        send(out_buf.at[p], far_rows(me), far_send, far_recv, (pd, pw))

    cuts = [0, 1, doms // 4, doms]
    for_peers(dom, work, doms, works, answer, cuts[0], cuts[1])
    landed(0, 0, 1)
    hop([rows(0, line, z * SIDE, SIDE)], 0, 1, along_z)
    landed(1, 0, 1)
    hop([rows(1, y, dom, 1) for y in range(lines)], 1, 1, along_x)
    for_peers(dom, work, doms, works, answer, cuts[1], cuts[2])
    landed(0, 1, SIDE)
    hop([rows(0, line, 0, doms)], 0, 2, along_y)
    landed(1, 1, lines)
    hop([rows(1, y, z * SIDE, SIDE) for y in range(lines)], 1, 2, along_z)
    for_peers(dom, work, doms, works, answer, cuts[2], cuts[3])

    load.wait()

    def pick(b):
        def one(e, carry):
            rel_ref[b * per_bucket + e] = relv[ids_ref[b, e]]
            return carry

        lax.fori_loop(0, per_bucket, one, 0, unroll=8)

    for b in range(buckets - 1):
        pick(b)

    landed(0, 2, doms)
    landed(1, 2, lines * SIDE)
    for y in range(lines):
        mine = w_ref.at[pl.ds((y * 2 + core) * own, own)]
        send(mine, mine, x_send, x_recv, (dom, line * 2 + 1 - core))
    pick(buckets - 1)

    for i in range(steps):
        spot = slice(i % tiles * edges, (i % tiles + 1) * edges)
        slot_v[2 * i] = src_v[i // tiles:i // tiles + 1, spot]
        slot_v[2 * i + 1] = tgt_v[i // tiles:i // tiles + 1, spot]

    high = lax.broadcasted_iota(jnp.int32, (16, negs), 0)
    low = lax.broadcasted_iota(jnp.int32, (128, negs), 0)
    for b in range(buckets):
        for side in range(2):
            slot = neg_ref[b, side:side + 1, :]
            top = (high == lax.shift_right_logical(slot, 7)).astype(F32).astype(BF16)
            end = (low == jnp.bitwise_and(slot, 127)).astype(F32).astype(BF16)
            table = lax.dot_general(end, top, NT, preferred_element_type=F32) * (0.5 / negs)
            for g in range(slots // 128):
                cnt[b * 2 + side, cols(g), :] = jnp.broadcast_to(table[:, g:g + 1], (128, 128))

    swapped = w_ref.at[pl.ds(0, hub // 2)]
    arrived(swapped, x_recv)

    def narrow(first, end):
        for c in range(4):
            column = w_ref[first:end, c, :]
            wb[first:end, cols(c)] = column.astype(BF16)
            wbt[cols(c), first:end] = column.T.astype(BF16)

    narrow(0, hub)
    arrived(w_ref.at[pl.ds(hub, count * CAP)], far_recv)

    narrow(hub, slots)

    block = 128
    eighth = own // doms
    msg = CAP * 4
    acc, theirs, mine, qf = (relv.at[pl.ds(k * lines * own, lines * own), :] for k in range(4))

    def gather(i, at, n):
        b, first = i // tiles, lax.rem(i, tiles) * edges + at
        place = (lax.rem(i, 2) * edges + at) * 4
        for e in range(n):
            to = pl.ds(pl.multiple_of(place + e * 4, 4), 4)
            hlin[to, :] = w_ref[source_s[b, first + e]]
            tlin[to, :] = w_ref[target_s[b, first + e]]

    def gather_first(k, carry):
        gather(0, k * 16, 16)
        return carry

    lax.fori_loop(0, edges // 16, gather_first, 0)

    def step(i, carry):
        b = i // tiles
        base = i * edges
        coming = lax.rem(i + 1, steps)

        held = lax.rem(i, 2) * edges

        def forward(k, carry):
            row = pl.multiple_of(k * block, block)
            here = pl.ds(row, block)
            there = pl.ds(pl.multiple_of(base + row, block), block)
            query = pl.ds(pl.multiple_of(2 * base + row, block), block)
            mirror = pl.ds(pl.multiple_of(2 * base + edges + row, block), block)
            score = jnp.zeros((block, 128), F32)
            for p in range(2):
                q = p + 2
                hr, hi = (hlin[pl.ds(4 * (held + row) + c, block, stride=4), :] for c in (p, q))
                tr, ti = (tlin[pl.ds(4 * (held + row) + c, block, stride=4), :] for c in (p, q))
                rr, ri = rel_ref[there, cols(p)], rel_ref[there, cols(q)]
                qr = hr * rr - hi * ri
                qi = hr * ri + hi * rr
                score = score + (qr * tr + qi * ti)
                qf[here, cols(p)] = qr
                qf[here, cols(q)] = qi
                rneg[query, cols(p)] = qr.astype(BF16)
                rneg[query, cols(q)] = qi.astype(BF16)
                rneg[mirror, cols(p)] = (rr * tr + ri * ti).astype(BF16)
                rneg[mirror, cols(q)] = (rr * ti - ri * tr).astype(BF16)
            positive = jnp.sum(score, axis=1, keepdims=True)
            slope_v[here, :] = jnp.broadcast_to(0.5 * jnp.tanh(0.5 * positive) - 0.5, (block, 128))
            return carry

        lax.fori_loop(0, edges // block, forward, 0)

        def score(side, carry):
            there = pl.ds(pl.multiple_of(2 * base + side * edges, edges), edges)
            parts = slots // 512
            few = edges // 2 // (parts + 1)
            for m in range(parts):
                rows = slice(m * 512, (m + 1) * 512)
                st = lax.dot_general(wb[rows, :], rneg[there, :], NT, preferred_element_type=F32)
                gather(coming, side * (edges // 2) + m * few, few)
                weight = cnt[b * 2 + 1 - side, rows, :]
                weight = jnp.concatenate([weight] * (edges // 128), axis=1)
                gt[rows, there] = (weight * jnp.tanh(0.5 * st) + weight).astype(BF16)
            gather(coming, side * (edges // 2) + parts * few, few)
            dneg[side] = jnp.dot(wbt[...], gt[:, there], preferred_element_type=F32)
            return carry

        score(0, 0)
        score(1, 0)

        def backward(k, carry):
            row = pl.multiple_of(k * block, block)
            here = pl.ds(row, block)
            there = pl.ds(pl.multiple_of(base + row, block), block)
            source = pl.ds(pl.multiple_of(2 * base + row, block), block)
            target = pl.ds(pl.multiple_of(2 * base + edges + row, block), block)

            def put(at, c, value):
                top = value.astype(BF16)
                rhi[at, cols(c)] = top
                rlo[at, cols(c)] = ((value - top.astype(F32)) * LOW).astype(F8)

            slope = slope_v[here, :]
            for p in range(2):
                q = p + 2
                rr, ri = rel_ref[there, cols(p)], rel_ref[there, cols(q)]
                tr, ti = (tlin[pl.ds(4 * (held + row) + c, block, stride=4), :] for c in (p, q))
                dqr = slope * tr + dneg[0, cols(p), here].T
                dqi = slope * ti + dneg[0, cols(q), here].T
                put(source, p, dqr * rr + dqi * ri)
                put(source, q, dqi * rr - dqr * ri)
                dur = dneg[1, cols(p), here].T
                dui = dneg[1, cols(q), here].T
                put(target, p, slope * qf[here, cols(p)] + (dur * rr - dui * ri))
                put(target, q, slope * qf[here, cols(q)] + (dur * ri + dui * rr))
            return carry

        lax.fori_loop(0, edges // block, backward, 0)
        return carry

    lax.fori_loop(0, steps, step, 0)

    def gradient(starts, beside):
        acc[...] = jnp.zeros(acc.shape, F32)

        def chunk(k, carry):
            at = pl.ds(pl.multiple_of(k * edges, edges), edges)
            slot = slot_v[k]
            number = lax.broadcasted_iota(jnp.int32, (own, edges), 0)
            hot = jnp.concatenate(
                [(number == slot - start).astype(F32).astype(BF16) for start in starts], axis=0
            )
            weight = jnp.concatenate([gt[pl.ds(start, own), at] for start in starts], axis=0)
            low = jnp.dot(hot.astype(F8), rlo[at, :], preferred_element_type=F32)
            acc[...] += (
                jnp.dot(weight, rneg[at, :], preferred_element_type=F32)
                + jnp.dot(hot, rhi[at, :], preferred_element_type=F32)
                + low * (1.0 / LOW)
            )
            beside(k)
            return carry

        lax.fori_loop(0, 2 * steps, chunk, 0)

    gradient([hub + j * own for j in range(count * CAP // own)], lambda k: None)
    for c in range(4):
        far_lin[pl.ds(c, count * CAP, stride=4), :] = acc[:, cols(c)]
    def far_grads(p):
        return far_lin.at[pl.ds(pl.multiple_of(p * msg, msg), msg), :]

    pltpu.make_async_copy(far_grads(me), back.at[me], back_recv).start()
    share = count // (4 * steps)

    def give(from_step):
        def some(k):
            for n in range(share):
                i = (from_step + k) * share + n

                @pl.when(i > 0)
                def _():
                    pd, pw = ring(dom, i // works, doms), ring(work, lax.rem(i, works), works)
                    send(far_grads(pd * works + pw), back.at[me], back_send, back_recv, (pd, pw))

        return some

    def starts(of):
        return [pl.multiple_of((y * 2 + of) * own, own) for y in range(lines)]

    gradient(starts(1 - core), give(0))
    theirs[...] = acc[...]
    for y in range(lines):
        send(theirs.at[pl.ds(y * own, own), :], xbuf.at[y], y_send, y_recv.at[y], (dom, line * 2 + 1 - core))
    gradient(starts(core), give(2 * steps))

    for y in range(lines):
        arrived(xbuf.at[y], y_recv.at[y])
        mine[pl.ds(y * own, own), :] = acc[pl.ds(y * own, own), :] + xbuf[y]

    def piece(y, d):
        return mine.at[pl.ds(pl.multiple_of(y * own + d * eighth, eighth), eighth), :]

    slot = dom * lines + line
    pltpu.make_async_copy(piece(line, dom), r2.at[slot], r2_recv).start()

    def scatter(i, carry):
        pd, py = ring(dom, i // lines, doms), ring(line, lax.rem(i, lines), lines)
        send(piece(py, pd), r2.at[slot], r2_send, r2_recv, (pd, py * 2 + core))
        return carry

    lax.fori_loop(1, doms * lines, scatter, 0)

    want_t[...] = want_ref[:, 0, :].T
    arrived(back, back_recv)
    row = lax.broadcasted_iota(jnp.int32, (own, count), 0)
    flat = back.reshape(count * msg, 128)
    sums = [jnp.zeros((own, 128), F32) for _ in range(4)]
    for c in range(CAP):
        hot = (row == want_t[pl.ds(lane + c, 1), :]).astype(F32)
        for k in range(4):
            got = flat[pl.ds(c * 4 + k, count, stride=msg), :]
            sums[k] += jnp.dot(hot, got, preferred_element_type=F32, precision=lax.Precision.HIGHEST)
    for k in range(4):
        acc[0:own, cols(k)] = sums[k]

    arrived(r2, r2_recv)
    total[...] = jnp.sum(r2[...], axis=0)
    pltpu.make_async_copy(total, r3.at[dom], r3_recv).start()

    def hand(i, carry):
        send(total, r3.at[dom], r3_send, r3_recv, (ring(dom, i, doms), work))
        return carry

    lax.fori_loop(1, doms, hand, 0)
    arrived(r3, r3_recv)
    owner = dom == hub_ref[0]
    hub_sum = r3[...].reshape(own, width)
    grads = [acc[0:own, cols(k)] + jnp.where(owner, hub_sum[:, cols(k)], 0.0) for k in range(4)]
    square = sum(g * g for g in grads)
    mean = jnp.sum(square, axis=1, keepdims=True) * (1.0 / width)
    old = jnp.broadcast_to(state_ref[...], (128, own)).T
    new = old + mean
    scale = 0.1 / (jnp.sqrt(new) + 1e-10)
    for k, g in enumerate(grads):
        rows_out[:, cols(k)] = ent_ref[:, cols(k)] - g * scale
    state_out[...] = new.T[0:1, :]

    arrived(xbuf, y_send)
    arrived(back.at[pl.ds(0, count - 1)], back_send)
    arrived(r2.at[pl.ds(0, doms * lines - 1)], r2_send)
    arrived(r3.at[pl.ds(0, doms - 1)], r3_send)
    arrived(swapped, x_send)
    arrived(w_ref.at[pl.ds(0, 2 * (doms * lines - 1) * part)], h2_send)
    arrived(hub1.at[:, pl.ds(0, doms - 1)], h1_send)
    arrived(out_buf.at[pl.ds(0, count - 1)], far_send)
    arrived(want_ref.at[pl.ds(0, count - 1)], req_send)


def window(doms, works, entity_rows, state, relations, hub_part, requests, source, relation_ids, target, negative,
           edges=512):
    own, width = entity_rows.shape
    count = doms * works
    lines = works // 2
    part = own // 2 // doms
    eighth = own // doms
    slots = works * own + count * CAP
    total = source.size
    any_, smem = pl.BlockSpec(memory_space=pl.ANY), pl.BlockSpec(memory_space=pltpu.SMEM)
    vmem = pl.BlockSpec(memory_space=pltpu.VMEM)
    dma = pltpu.SemaphoreType.DMA
    i32 = jnp.int32
    return pl.pallas_call(
        functools.partial(window_kernel, doms, works, edges),
        in_specs=[smem] * 4 + [any_] * 7,
        out_specs=[vmem, vmem],
        out_shape=[
            jax.ShapeDtypeStruct((own, width), F32),
            jax.ShapeDtypeStruct((1, own), F32),
        ],
        scratch_shapes=[
            pltpu.VMEM((own, width), F32),
            pltpu.VMEM(requests.shape, i32),
            pltpu.VMEM(source.shape, i32),
            pltpu.VMEM(target.shape, i32),
            pltpu.VMEM(negative.shape, i32),
            pltpu.VMEM(state.shape, F32),
            pltpu.VMEM((slots, 4, 128), F32),
            pltpu.VMEM((count, 1, 128), i32),
            pltpu.VMEM((total, width), F32),
            pltpu.VMEM((own, 4, 128), F32),
            pltpu.VMEM((2, doms, part, 4, 128), F32),
            pltpu.VMEM((count, CAP, 4, 128), F32),
            pltpu.VMEM((count * CAP // 128, 1, 128), i32),
            pltpu.SMEM((count, 1, 128), i32),
            pltpu.VMEM(relations.shape, F32),
            pltpu.VMEM((slots, width), BF16),
            pltpu.VMEM((width, slots), BF16),
            pltpu.VMEM((2 * source.shape[0], slots, 128), F32),
            pltpu.VMEM((2 * total // edges, 1, edges), i32),
            pltpu.VMEM((slots, 2 * total), BF16),
            pltpu.VMEM((2 * total, width), BF16),
            pltpu.VMEM((2 * total, width), BF16),
            pltpu.VMEM((2 * total, width), F8),
            pltpu.VMEM((2 * edges * 4, 128), F32),
            pltpu.VMEM((2 * edges * 4, 128), F32),
            pltpu.VMEM((edges, 128), F32),
            pltpu.VMEM((2, width, edges), F32),
            pltpu.VMEM((count * CAP * 4, 128), F32),
            pltpu.VMEM((count, CAP * 4, 128), F32),
            pltpu.VMEM((lines, own, width), F32),
            pltpu.VMEM((doms * lines, eighth, width), F32),
            pltpu.VMEM((eighth, width), F32),
            pltpu.VMEM((doms, eighth, width), F32),
            pltpu.VMEM((128, count), i32),
            dma((6,)), dma, dma, dma, dma, dma, dma, dma, dma((2, 3)), dma, dma, dma, dma,
            dma, dma((lines,)), dma, dma, dma, dma, dma, dma,
        ],
        compiler_params=pltpu.CompilerParams(
            collective_id=0, has_side_effects=True, vmem_limit_bytes=60 * MIB
        ),
        name="window",
    )(hub_part, relation_ids, source, target, entity_rows, requests, relations, source, target, negative, state)


def per_device(doms, works, entity_rows, adagrad_state, *others):
    own = entity_rows.shape[0]
    new_rows, new_state = window(doms, works, entity_rows, adagrad_state.reshape(1, own), *others)
    return new_rows, new_state.reshape(own)


def solution(mesh):
    doms, works = mesh.shape["dom"], mesh.shape["work"]
    both = ("dom", "work")
    return jax.shard_map(
        functools.partial(per_device, doms, works),
        mesh=mesh,
        in_specs=(
            P(both, None), P(both), P(), P(), P(both, None), P(both, None),
            P(both, None), P(both, None), P(both, None, None),
        ),
        out_specs=(P(both, None), P(both)),
        check_vma=False,
    )
```

```python
import functools
import jax
import jax.numpy as jnp
from jax import lax
from jax.experimental import pallas as pl
from jax.experimental.pallas import tpu as pltpu
from jax.sharding import PartitionSpec as P

F32 = jnp.float32
BF16 = jnp.bfloat16
F8 = jnp.float8_e4m3fn
LOW = 1024.0
NT = (((1,), (1,)), ((), ()))
MESH = pl.DeviceIdType.MESH
MIB = 1024 * 1024
CAP = 4
SIDE = 4


def ring(at, by, size):
    return lax.rem(at + by, size)


def for_peers(dom, work, doms, works, act, first=0, last=None):
    near = [ring(work, k, works) for k in range(works)]
    if first == 0:
        for pw in near[1:]:
            act(dom, pw)

    def along(i, carry):
        pd = ring(dom, i, doms)
        for pw in near:
            act(pd, pw)
        return carry

    lax.fori_loop(max(first, 1), last or doms, along, 0)


def greet(doms, works):
    dom, work = lax.axis_index("dom"), lax.axis_index("work")
    barrier = pltpu.get_barrier_semaphore()

    def call(pd, pw):
        pl.semaphore_signal(barrier, inc=1, device_id=(pd, pw), device_id_type=MESH)

    for_peers(dom, work, doms, works, call)


def greeted(doms, works):
    pl.semaphore_wait(pltpu.get_barrier_semaphore(), doms * works - 1)


def arrived(ref, sem):
    pltpu.make_async_copy(ref, ref, sem).wait()


def send(src, dst, sent, landed, device):
    pltpu.make_async_remote_copy(
        src_ref=src, dst_ref=dst, send_sem=sent, recv_sem=landed, device_id=device, device_id_type=MESH
    ).start()


def cols(c):
    return slice(c * 128, (c + 1) * 128)


def window_kernel(doms, works, edges, hub_ref, ids_ref, source_s, target_s, ent_hbm, req_hbm, rel_hbm,
                  src_hbm, tgt_hbm, neg_hbm, state_hbm,
                  rows_out, state_out,
                  ent_ref, req_ref, src_v, tgt_v, neg_ref, state_ref,
                  w_ref, want_ref, rel_ref, erow, hub1, out_buf, reqv, want_s, relv,
                  wb, wbt, cnt, slot_v, gt, rneg, rhi, rlo, hlin, tlin, slope_v, dneg,
                  far_lin, back, xbuf, r2, total, r3, want_t,
                  in_sem, rel_sem, req_send, req_recv, loc_sem, h1_send, h1_recv, h2_send, h2_recv,
                  x_send, x_recv, far_send, far_recv,
                  y_send, y_recv, back_send, back_recv, r2_send, r2_recv, r3_send, r3_recv):
    dom, work = lax.axis_index("dom"), lax.axis_index("work")
    me = dom * works + work
    core, line = lax.rem(work, 2), work // 2
    z, x = dom // SIDE, lax.rem(dom, SIDE)
    lines = works // 2
    count = doms * works
    own = ent_ref.shape[0]
    half = own // 2
    part = half // doms
    hub = works * own
    per_row = 128 // CAP
    buckets, per_bucket = ids_ref.shape
    width = ent_ref.shape[1]
    slots = wb.shape[0]
    negs = neg_ref.shape[2]
    tiles = per_bucket // edges
    steps = buckets * tiles

    load = pltpu.make_async_copy(rel_hbm, relv, rel_sem)
    moves = [
        pltpu.make_async_copy(src, dst, in_sem.at[i]) for i, (src, dst) in enumerate((
            (ent_hbm, ent_ref), (req_hbm, req_ref), (src_hbm, src_v), (tgt_hbm, tgt_v), (neg_hbm, neg_ref),
            (state_hbm, state_ref),
        ))
    ]
    for move in moves:
        move.start()
    load.start()
    greet(doms, works)
    for move in moves:
        move.wait()
    for c in range(4):
        erow[:, c, :] = ent_ref[:, cols(c)]
    for j in range(count // per_row):
        reqv[j] = req_ref[:, cols(j)]
    greeted(doms, works)

    for s in range(2):
        hub1[s, dom] = erow[pl.ds(s * half + dom * part, part)]

    def spread(i, carry):
        pd = ring(dom, i, doms)
        for s in range(2):
            send(erow.at[pl.ds(s * half + pd * part, part)], hub1.at[s, dom], h1_send, h1_recv, (pd, work))
        return carry

    lax.fori_loop(1, doms, spread, 0)

    want_ref[me] = reqv[me // per_row]

    def ask(pd, pw):
        send(reqv.at[(pd * works + pw) // per_row], want_ref.at[me], req_send, req_recv, (pd, pw))

    for_peers(dom, work, doms, works, ask)

    def rows(s, y, d, n):
        return w_ref.at[pl.ds((y * 2 + core) * own + s * half + d * part, n * part)]

    def along_x(k):
        return (z * SIDE + ring(x, k, SIDE), work)

    def along_z(k):
        return (ring(z, k, SIDE) * SIDE + x, work)

    def along_y(k):
        return (dom, ring(line, k, lines) * 2 + core)

    around = (1, SIDE - 1, 2)

    def hop(refs, s, step, to):
        for k in around:
            for ref in refs:
                send(ref, ref, h2_send, h2_recv.at[s, step], to(k))

    def landed(s, step, n):
        arrived(w_ref.at[pl.ds(0, (SIDE - 1) * n * part)], h2_recv.at[s, step])

    arrived(hub1.at[:, pl.ds(0, doms - 1)], h1_recv)
    at = hub_ref[0]
    for s in range(2):
        w_ref[pl.ds((line * 2 + core) * own + s * half + dom * part, part)] = hub1[s, at]
    hop([rows(0, line, dom, 1)], 0, 0, along_x)
    hop([rows(1, line, dom, 1)], 1, 0, along_y)

    arrived(want_ref.at[pl.ds(0, count - 1)], req_recv)
    copy = pltpu.make_async_copy(want_ref, want_s, loc_sem)
    copy.start()
    copy.wait()
    lane = lax.rem(me, per_row) * CAP

    def fill(p):
        for c in range(CAP):
            out_buf[p, c] = erow[want_s[p, 0, lane + c]]

    def far_rows(p):
        return w_ref.at[pl.ds(hub + p * CAP, CAP)]

    fill(me)
    pltpu.make_async_copy(out_buf.at[me], far_rows(me), far_recv).start()

    def answer(pd, pw):
        p = pd * works + pw
        fill(p)
        send(out_buf.at[p], far_rows(me), far_send, far_recv, (pd, pw))

    cuts = [0, 1, doms // 4, doms]
    for_peers(dom, work, doms, works, answer, cuts[0], cuts[1])
    landed(0, 0, 1)
    hop([rows(0, line, z * SIDE, SIDE)], 0, 1, along_z)
    landed(1, 0, 1)
    hop([rows(1, y, dom, 1) for y in range(lines)], 1, 1, along_x)
    for_peers(dom, work, doms, works, answer, cuts[1], cuts[2])
    landed(0, 1, SIDE)
    hop([rows(0, line, 0, doms)], 0, 2, along_y)
    landed(1, 1, lines)
    hop([rows(1, y, z * SIDE, SIDE) for y in range(lines)], 1, 2, along_z)
    for_peers(dom, work, doms, works, answer, cuts[2], cuts[3])

    load.wait()

    def pick(b):
        def one(e, carry):
            rel_ref[b * per_bucket + e] = relv[ids_ref[b, e]]
            return carry

        lax.fori_loop(0, per_bucket, one, 0, unroll=8)

    for b in range(buckets - 1):
        pick(b)

    landed(0, 2, doms)
    landed(1, 2, lines * SIDE)
    for y in range(lines):
        mine = w_ref.at[pl.ds((y * 2 + core) * own, own)]
        send(mine, mine, x_send, x_recv, (dom, line * 2 + 1 - core))
    pick(buckets - 1)

    for i in range(steps):
        spot = slice(i % tiles * edges, (i % tiles + 1) * edges)
        slot_v[2 * i] = src_v[i // tiles:i // tiles + 1, spot]
        slot_v[2 * i + 1] = tgt_v[i // tiles:i // tiles + 1, spot]

    high = lax.broadcasted_iota(jnp.int32, (16, negs), 0)
    low = lax.broadcasted_iota(jnp.int32, (128, negs), 0)
    for b in range(buckets):
        for side in range(2):
            slot = neg_ref[b, side:side + 1, :]
            top = (high == lax.shift_right_logical(slot, 7)).astype(F32).astype(BF16)
            end = (low == jnp.bitwise_and(slot, 127)).astype(F32).astype(BF16)
            table = lax.dot_general(end, top, NT, preferred_element_type=F32) * (0.5 / negs)
            for g in range(slots // 128):
                cnt[b * 2 + side, cols(g), :] = jnp.broadcast_to(table[:, g:g + 1], (128, 128))

    swapped = w_ref.at[pl.ds(0, hub // 2)]
    arrived(swapped, x_recv)

    def narrow(first, end):
        for c in range(4):
            column = w_ref[first:end, c, :]
            wb[first:end, cols(c)] = column.astype(BF16)
            wbt[cols(c), first:end] = column.T.astype(BF16)

    narrow(0, hub)
    arrived(w_ref.at[pl.ds(hub, count * CAP)], far_recv)

    narrow(hub, slots)

    block = 128
    eighth = own // doms
    msg = CAP * 4
    acc, theirs, mine, qf = (relv.at[pl.ds(k * lines * own, lines * own), :] for k in range(4))

    def gather(i, at, n):
        b, first = i // tiles, lax.rem(i, tiles) * edges + at
        place = (lax.rem(i, 2) * edges + at) * 4
        for e in range(n):
            to = pl.ds(pl.multiple_of(place + e * 4, 4), 4)
            hlin[to, :] = w_ref[source_s[b, first + e]]
            tlin[to, :] = w_ref[target_s[b, first + e]]

    def gather_first(k, carry):
        gather(0, k * 16, 16)
        return carry

    lax.fori_loop(0, edges // 16, gather_first, 0)

    def step(i, carry):
        b = i // tiles
        base = i * edges
        coming = lax.rem(i + 1, steps)

        held = lax.rem(i, 2) * edges

        def forward(k):
            row = k * block
            here = pl.ds(row, block)
            there = pl.ds(pl.multiple_of(base + row, block), block)
            query = pl.ds(pl.multiple_of(2 * base + row, block), block)
            mirror = pl.ds(pl.multiple_of(2 * base + edges + row, block), block)
            score = jnp.zeros((block, 128), F32)
            for p in range(2):
                q = p + 2
                hr, hi = (hlin[pl.ds(4 * (held + row) + c, block, stride=4), :] for c in (p, q))
                tr, ti = (tlin[pl.ds(4 * (held + row) + c, block, stride=4), :] for c in (p, q))
                rr, ri = rel_ref[there, cols(p)], rel_ref[there, cols(q)]
                qr = hr * rr - hi * ri
                qi = hr * ri + hi * rr
                score = score + (qr * tr + qi * ti)
                qf[here, cols(p)] = qr
                qf[here, cols(q)] = qi
                rneg[query, cols(p)] = qr.astype(BF16)
                rneg[query, cols(q)] = qi.astype(BF16)
                rneg[mirror, cols(p)] = (rr * tr + ri * ti).astype(BF16)
                rneg[mirror, cols(q)] = (rr * ti - ri * tr).astype(BF16)
            positive = jnp.sum(score, axis=1, keepdims=True)
            slope_v[here, :] = jnp.broadcast_to(0.5 * jnp.tanh(0.5 * positive) - 0.5, (block, 128))

        for k in range(edges // block):
            forward(k)

        def score(side, carry):
            there = pl.ds(pl.multiple_of(2 * base + side * edges, edges), edges)
            parts = slots // 512
            few = edges // 2 // (parts + 1)
            for m in range(parts):
                rows = slice(m * 512, (m + 1) * 512)
                st = lax.dot_general(wb[rows, :], rneg[there, :], NT, preferred_element_type=F32)
                gather(coming, side * (edges // 2) + m * few, few)
                weight = cnt[b * 2 + 1 - side, rows, :]
                weight = jnp.concatenate([weight] * (edges // 128), axis=1)
                gt[rows, there] = (weight * jnp.tanh(0.5 * st) + weight).astype(BF16)
            gather(coming, side * (edges // 2) + parts * few, few)
            dneg[side] = jnp.dot(wbt[...], gt[:, there], preferred_element_type=F32)
            return carry

        score(0, 0)
        score(1, 0)

        def backward(k, carry):
            row = pl.multiple_of(k * block, block)
            here = pl.ds(row, block)
            there = pl.ds(pl.multiple_of(base + row, block), block)
            source = pl.ds(pl.multiple_of(2 * base + row, block), block)
            target = pl.ds(pl.multiple_of(2 * base + edges + row, block), block)

            def put(at, c, value):
                top = value.astype(BF16)
                rhi[at, cols(c)] = top
                rlo[at, cols(c)] = ((value - top.astype(F32)) * LOW).astype(F8)

            slope = slope_v[here, :]
            for p in range(2):
                q = p + 2
                rr, ri = rel_ref[there, cols(p)], rel_ref[there, cols(q)]
                tr, ti = (tlin[pl.ds(4 * (held + row) + c, block, stride=4), :] for c in (p, q))
                dqr = slope * tr + dneg[0, cols(p), here].T
                dqi = slope * ti + dneg[0, cols(q), here].T
                put(source, p, dqr * rr + dqi * ri)
                put(source, q, dqi * rr - dqr * ri)
                dur = dneg[1, cols(p), here].T
                dui = dneg[1, cols(q), here].T
                put(target, p, slope * qf[here, cols(p)] + (dur * rr - dui * ri))
                put(target, q, slope * qf[here, cols(q)] + (dur * ri + dui * rr))
            return carry

        lax.fori_loop(0, edges // block, backward, 0)
        return carry

    lax.fori_loop(0, steps, step, 0)

    def gradient(starts, beside):
        acc[...] = jnp.zeros(acc.shape, F32)

        def chunk(k, carry):
            at = pl.ds(pl.multiple_of(k * edges, edges), edges)
            slot = slot_v[k]
            number = lax.broadcasted_iota(jnp.int32, (own, edges), 0)
            hot = jnp.concatenate(
                [(number == slot - start).astype(F32).astype(BF16) for start in starts], axis=0
            )
            weight = jnp.concatenate([gt[pl.ds(start, own), at] for start in starts], axis=0)
            low = jnp.dot(hot.astype(F8), rlo[at, :], preferred_element_type=F32)
            acc[...] += (
                jnp.dot(weight, rneg[at, :], preferred_element_type=F32)
                + jnp.dot(hot, rhi[at, :], preferred_element_type=F32)
                + low * (1.0 / LOW)
            )
            beside(k)
            return carry

        lax.fori_loop(0, 2 * steps, chunk, 0)

    gradient([hub + j * own for j in range(count * CAP // own)], lambda k: None)
    for c in range(4):
        far_lin[pl.ds(c, count * CAP, stride=4), :] = acc[:, cols(c)]
    def far_grads(p):
        return far_lin.at[pl.ds(pl.multiple_of(p * msg, msg), msg), :]

    pltpu.make_async_copy(far_grads(me), back.at[me], back_recv).start()
    loops = 2 * steps

    def give(pd, pw):
        send(far_grads(pd * works + pw), back.at[me], back_send, back_recv, (pd, pw))

    def give_group(k):
        for pw in near:
            give(ring(dom, k + 1, doms), pw)

    share = (doms - 1 - loops) * works // loops

    def give_share(k):
        for n in range(share):
            i = k * share + n
            give(ring(dom, loops + 1 + i // works, doms), ring(work, lax.rem(i, works), works))

    near = [ring(work, k, works) for k in range(works)]
    for pw in near[1:]:
        give(dom, pw)

    def starts(of):
        return [pl.multiple_of((y * 2 + of) * own, own) for y in range(lines)]

    gradient(starts(1 - core), give_group)
    theirs[...] = acc[...]
    for y in range(lines):
        send(theirs.at[pl.ds(y * own, own), :], xbuf.at[y], y_send, y_recv.at[y], (dom, line * 2 + 1 - core))
    gradient(starts(core), give_share)

    for y in range(lines):
        arrived(xbuf.at[y], y_recv.at[y])
        mine[pl.ds(y * own, own), :] = acc[pl.ds(y * own, own), :] + xbuf[y]

    def piece(y, d):
        return mine.at[pl.ds(pl.multiple_of(y * own + d * eighth, eighth), eighth), :]

    slot = dom * lines + line
    pltpu.make_async_copy(piece(line, dom), r2.at[slot], r2_recv).start()

    spots = [ring(line, k, lines) for k in range(lines)]

    def scatter(pd, py):
        send(piece(py, pd), r2.at[slot], r2_send, r2_recv, (pd, py * 2 + core))

    for py in spots[1:]:
        scatter(dom, py)

    def scatter_along(i, carry):
        for py in spots:
            scatter(ring(dom, i, doms), py)
        return carry

    lax.fori_loop(1, doms, scatter_along, 0)

    want_t[...] = want_ref[:, 0, :].T
    arrived(back, back_recv)
    row = lax.broadcasted_iota(jnp.int32, (own, count), 0)
    flat = back.reshape(count * msg, 128)
    sums = [jnp.zeros((own, 128), F32) for _ in range(4)]
    for c in range(CAP):
        hot = (row == want_t[pl.ds(lane + c, 1), :]).astype(F32)
        for k in range(4):
            got = flat[pl.ds(c * 4 + k, count, stride=msg), :]
            sums[k] += jnp.dot(hot, got, preferred_element_type=F32, precision=lax.Precision.HIGHEST)
    for k in range(4):
        acc[0:own, cols(k)] = sums[k]

    arrived(r2, r2_recv)
    total[...] = jnp.sum(r2[...], axis=0)
    pltpu.make_async_copy(total, r3.at[dom], r3_recv).start()

    def hand(i, carry):
        send(total, r3.at[dom], r3_send, r3_recv, (ring(dom, i, doms), work))
        return carry

    lax.fori_loop(1, doms, hand, 0)
    arrived(r3, r3_recv)
    owner = dom == hub_ref[0]
    hub_sum = r3[...].reshape(own, width)
    grads = [acc[0:own, cols(k)] + jnp.where(owner, hub_sum[:, cols(k)], 0.0) for k in range(4)]
    square = sum(g * g for g in grads)
    mean = jnp.sum(square, axis=1, keepdims=True) * (1.0 / width)
    old = jnp.broadcast_to(state_ref[...], (128, own)).T
    new = old + mean
    scale = 0.1 / (jnp.sqrt(new) + 1e-10)
    for k, g in enumerate(grads):
        rows_out[:, cols(k)] = ent_ref[:, cols(k)] - g * scale
    state_out[...] = new.T[0:1, :]

    arrived(xbuf, y_send)
    arrived(back.at[pl.ds(0, count - 1)], back_send)
    arrived(r2.at[pl.ds(0, doms * lines - 1)], r2_send)
    arrived(r3.at[pl.ds(0, doms - 1)], r3_send)
    arrived(swapped, x_send)
    arrived(w_ref.at[pl.ds(0, 2 * (doms * lines - 1) * part)], h2_send)
    arrived(hub1.at[:, pl.ds(0, doms - 1)], h1_send)
    arrived(out_buf.at[pl.ds(0, count - 1)], far_send)
    arrived(want_ref.at[pl.ds(0, count - 1)], req_send)


def window(doms, works, entity_rows, state, relations, hub_part, requests, source, relation_ids, target, negative,
           edges=512):
    own, width = entity_rows.shape
    count = doms * works
    lines = works // 2
    part = own // 2 // doms
    eighth = own // doms
    slots = works * own + count * CAP
    total = source.size
    any_, smem = pl.BlockSpec(memory_space=pl.ANY), pl.BlockSpec(memory_space=pltpu.SMEM)
    vmem = pl.BlockSpec(memory_space=pltpu.VMEM)
    dma = pltpu.SemaphoreType.DMA
    i32 = jnp.int32
    return pl.pallas_call(
        functools.partial(window_kernel, doms, works, edges),
        in_specs=[smem] * 4 + [any_] * 7,
        out_specs=[vmem, vmem],
        out_shape=[
            jax.ShapeDtypeStruct((own, width), F32),
            jax.ShapeDtypeStruct((1, own), F32),
        ],
        scratch_shapes=[
            pltpu.VMEM((own, width), F32),
            pltpu.VMEM(requests.shape, i32),
            pltpu.VMEM(source.shape, i32),
            pltpu.VMEM(target.shape, i32),
            pltpu.VMEM(negative.shape, i32),
            pltpu.VMEM(state.shape, F32),
            pltpu.VMEM((slots, 4, 128), F32),
            pltpu.VMEM((count, 1, 128), i32),
            pltpu.VMEM((total, width), F32),
            pltpu.VMEM((own, 4, 128), F32),
            pltpu.VMEM((2, doms, part, 4, 128), F32),
            pltpu.VMEM((count, CAP, 4, 128), F32),
            pltpu.VMEM((count * CAP // 128, 1, 128), i32),
            pltpu.SMEM((count, 1, 128), i32),
            pltpu.VMEM(relations.shape, F32),
            pltpu.VMEM((slots, width), BF16),
            pltpu.VMEM((width, slots), BF16),
            pltpu.VMEM((2 * source.shape[0], slots, 128), F32),
            pltpu.VMEM((2 * total // edges, 1, edges), i32),
            pltpu.VMEM((slots, 2 * total), BF16),
            pltpu.VMEM((2 * total, width), BF16),
            pltpu.VMEM((2 * total, width), BF16),
            pltpu.VMEM((2 * total, width), F8),
            pltpu.VMEM((2 * edges * 4, 128), F32),
            pltpu.VMEM((2 * edges * 4, 128), F32),
            pltpu.VMEM((edges, 128), F32),
            pltpu.VMEM((2, width, edges), F32),
            pltpu.VMEM((count * CAP * 4, 128), F32),
            pltpu.VMEM((count, CAP * 4, 128), F32),
            pltpu.VMEM((lines, own, width), F32),
            pltpu.VMEM((doms * lines, eighth, width), F32),
            pltpu.VMEM((eighth, width), F32),
            pltpu.VMEM((doms, eighth, width), F32),
            pltpu.VMEM((128, count), i32),
            dma((6,)), dma, dma, dma, dma, dma, dma, dma, dma((2, 3)), dma, dma, dma, dma,
            dma, dma((lines,)), dma, dma, dma, dma, dma, dma,
        ],
        compiler_params=pltpu.CompilerParams(
            collective_id=0, has_side_effects=True, vmem_limit_bytes=60 * MIB
        ),
        name="window",
    )(hub_part, relation_ids, source, target, entity_rows, requests, relations, source, target, negative, state)


def per_device(doms, works, entity_rows, adagrad_state, *others):
    own = entity_rows.shape[0]
    new_rows, new_state = window(doms, works, entity_rows, adagrad_state.reshape(1, own), *others)
    return new_rows, new_state.reshape(own)


def solution(mesh):
    doms, works = mesh.shape["dom"], mesh.shape["work"]
    both = ("dom", "work")
    return jax.shard_map(
        functools.partial(per_device, doms, works),
        mesh=mesh,
        in_specs=(
            P(both, None), P(both), P(), P(), P(both, None), P(both, None),
            P(both, None), P(both, None), P(both, None, None),
        ),
        out_specs=(P(both, None), P(both)),
        check_vma=False,
    )
```
